32 devices in a mesh: pts: 8 (over z, x), lmk: 4 (over y, core).
Axes of the slice: x: 2, y: 2, z: 4, core: 2. Of those that a mesh axis runs over, the one named last changes fastest.
Arguments:
- points: bfloat16 [12288, 768], P('pts'), may hold values from -8 to 8
- landmarks: bfloat16 [4096, 768], P(('pts', 'lmk')), may hold values from -8 to 8
- eigvecs: bfloat16 [4096, 128], P(('pts', 'lmk')), may hold values from -0.09375 to 0.09375
Outputs:
- spectral: float32 [12288, 128], P('pts')
The draws below stay inside these ranges and needn't reach their ends.
All inputs are finite; a program needn't handle non-finite values.
Results may differ from the reference program's by a relative error of at most 0.0076.
Values may be sent and summed in bfloat16 or wider, within the bound.
No kernel may reach another device: no remote copies, remote signals or barrier semaphores. Data moves between devices by JAX's collectives and lax.ppermute only.
A program may use at most 128 MiB of HBM per device.

```python
import math
import jax
import jax.numpy as jnp
from jax import lax

F = 768
K = 128
PTS_DEV = 1536
NP = 12288
NL = 4096
N_PTS = 8


def common_direction(key):
    return jnp.clip(jax.random.normal(key, (F,), jnp.float32), -3.0, 3.0)


def noise_rows(key, rows):
    return jnp.clip(jax.random.normal(key, (rows, F), jnp.float32), -5.0, 5.0)


def draw_points(key, part):
    direction = common_direction(key)
    key = jax.random.fold_in(key, 11)
    noise = noise_rows(key, NP)
    top = 0.25
    place = (jnp.arange(NP, dtype=jnp.float32) + 0.5) / NP
    weight = top * place
    return (noise + weight[:, None] * direction[None, :]).astype(jnp.bfloat16)


def draw_landmarks(key, part):
    direction = common_direction(key)
    key = jax.random.fold_in(key, 23)
    noise = noise_rows(key, NL)
    return (noise + 0.5 * direction[None, :]).astype(jnp.bfloat16)


def block_levels(stream_key, shape, split, least, largest):
    gain, own = 1.0, jax.random.fold_in(stream_key, 6)
    for dim, shards_of in split:
        draws = jnp.exp(jax.random.uniform(jax.random.fold_in(own, dim), (shards_of,), jnp.float32, least / len(split), largest / len(split)))
        gain = gain * jnp.repeat(draws, shape[dim] // shards_of).reshape([-1 if axis == dim else 1 for axis in range(len(shape))])
    return gain


def gaussian(stream_key, extent, scale, most, shards=(), kind=jnp.bfloat16):
    loudness = block_levels(stream_key, extent, shards, -0.22, 0.18) if shards else 1.0
    values = jax.random.normal(stream_key, extent, jnp.float32) * scale * loudness
    return jnp.minimum(jnp.maximum(values, -most), most).astype(kind)


def setup_inputs(seed: int = 0) -> dict:
    keys = jax.random.split(jax.random.key(seed), 4)
    return {
        "points": draw_points(jax.random.fold_in(keys[3], 71), 0),
        "landmarks": draw_landmarks(jax.random.fold_in(keys[3], 71), 0),
        "eigvecs": gaussian(keys[2], (NL, K), NL ** -0.5, 0.09375, ((0, 32),)),
    }


kernel_gain = 16.0

def unit_rows(values):
    floats = values.astype(jnp.float32)
    factor = lax.rsqrt(lax.optimization_barrier(jnp.mean(floats * floats, axis=-1, keepdims=True)) + 1e-06) / math.sqrt(values.shape[-1])
    return (floats * factor).astype(jnp.bfloat16)

def reference(points, landmarks, eigvecs):
    unit_land = unit_rows(landmarks).astype(jnp.float32)
    vectors = eigvecs.astype(jnp.float32)
    unit_pts = unit_rows(points)
    blocks = unit_pts.reshape(N_PTS, PTS_DEV, F)

    def one_block(block):
        cosine = jnp.dot(block.astype(jnp.float32), unit_land.T, precision=lax.Precision.HIGHEST)
        kernel = jnp.exp(2.0 * kernel_gain * (cosine - 1.0))
        degree = lax.optimization_barrier(jnp.sum(kernel, axis=1))
        kernel_b = lax.optimization_barrier(kernel.astype(jnp.bfloat16))
        projected = jnp.dot(kernel_b.astype(jnp.float32), vectors, precision=lax.Precision.HIGHEST)
        return projected / jnp.sqrt(degree)[:, None]
    embed = lax.map(one_block, blocks).reshape(NP, K)
    gram = jnp.dot(embed.T, embed, precision=lax.Precision.HIGHEST) / NP
    lower = jnp.linalg.cholesky(gram)
    return lax.linalg.triangular_solve(lower, embed, left_side=False, lower=True, transpose_a=True)
```

```python
import math

import jax
import jax.numpy as jnp
from jax import lax
from jax.sharding import PartitionSpec as P

kernel_gain = 16.0


def unit_rows(values):
    floats = values.astype(jnp.float32)
    factor = lax.rsqrt(jnp.mean(floats * floats, axis=-1, keepdims=True) + 1e-06) / math.sqrt(
        values.shape[-1]
    )
    return (floats * factor).astype(jnp.bfloat16)


def swap(value, axis, size, bit):
    return lax.ppermute(value, axis, [(i, i ^ bit) for i in range(size)])


def finish(embed, gram):
    lower = jnp.linalg.cholesky(gram)
    return lax.linalg.triangular_solve(lower, embed, left_side=False, lower=True, transpose_a=True)


def per_device(points, landmarks, eigvecs):
    num_pts = lax.axis_size("pts")
    num_lmk = lax.axis_size("lmk")
    num_rows = points.shape[0]
    features = points.shape[1]
    total_points = num_rows * num_pts
    half = num_rows // 2
    pts_bits = [1 << b for b in reversed(range(num_pts.bit_length() - 1))]
    lmk_bits = [1 << b for b in range(num_lmk.bit_length() - 1)]

    blocks = [jnp.concatenate([unit_rows(landmarks), eigvecs], axis=1)]
    unit_pts = unit_rows(points)
    degree, projected = 0.0, 0.0

    def meet(some):
        piece = jnp.concatenate(some, axis=0)
        cosine = lax.dot_general(
            unit_pts,
            piece[:, :features],
            (((1,), (1,)), ((), ())),
            preferred_element_type=jnp.float32,
        )
        kernel = jnp.exp(2.0 * kernel_gain * (cosine - 1.0))
        return jnp.sum(kernel, axis=1), jnp.dot(
            kernel.astype(jnp.bfloat16), piece[:, features:], preferred_element_type=jnp.float32
        )

    for bit in pts_bits:
        blocks = blocks + [swap(block, "pts", num_pts, bit) for block in blocks]
    for first in range(0, num_pts, 4):
        more = meet(blocks[first : first + 4])
        degree, projected = degree + more[0], projected + more[1]

    core = lax.axis_index("lmk") % 2
    own_rows = core * half
    other_rows = half - own_rows

    def rows_of(value, start):
        return lax.dynamic_slice_in_dim(value, start, half, 0)

    deg = rows_of(degree, own_rows) + swap(rows_of(degree, other_rows), "lmk", num_lmk, 1)
    proj = rows_of(projected, own_rows) + swap(rows_of(projected, other_rows), "lmk", num_lmk, 1)
    for bit in lmk_bits[1:]:
        deg = deg + swap(deg, "lmk", num_lmk, bit)
        proj = proj + swap(proj, "lmk", num_lmk, bit)
    embed = proj / jnp.sqrt(deg)[:, None]
    gram = jnp.dot(embed.T, embed, precision=lax.Precision.HIGHEST)
    other = swap(embed, "lmk", num_lmk, 1)
    gram = gram + swap(gram, "lmk", num_lmk, 1)
    for bit in pts_bits:
        gram = gram + swap(gram, "pts", num_pts, bit)
    gram = gram / total_points
    first = jnp.where(core == 0, embed, other)
    second = jnp.where(core == 0, other, embed)
    return finish(jnp.concatenate([first, second], axis=0), gram)


def solution(mesh):
    placed = (P("pts", None), P(("pts", "lmk"), None), P(("pts", "lmk"), None))
    return jax.shard_map(
        per_device, mesh=mesh, in_specs=placed, out_specs=P("pts", None), check_vma=False
    )
```

```python
import functools
import math

import jax
import jax.numpy as jnp
from jax import lax
from jax.experimental import pallas as pl
from jax.experimental.pallas import tpu as pltpu
from jax.sharding import PartitionSpec as P

kernel_gain = 16.0
LANES = 128
TILE = 256
PANEL = 16
VMEM = pl.BlockSpec(memory_space=pltpu.VMEM)
BF16 = jnp.bfloat16
F32 = jnp.float32


def unit_rows(values):
    floats = values.astype(F32)
    factor = lax.rsqrt(jnp.mean(floats * floats, axis=-1, keepdims=True) + 1e-06) / math.sqrt(
        values.shape[-1]
    )
    return (floats * factor).astype(BF16)


def split3(value):
    high = value.astype(BF16)
    rest = value - high.astype(F32)
    mid = rest.astype(BF16)
    low = (rest - mid.astype(F32)).astype(BF16)
    return high, mid, low


def swap(value, axis, size, bit):
    return lax.ppermute(value, axis, [(i, i ^ bit) for i in range(size)])


def eye(size):
    row = lax.broadcasted_iota(jnp.int32, (size, size), 0)
    column = lax.broadcasted_iota(jnp.int32, (size, size), 1)
    return row == column


def call_on(kernel, out, operands, **rest):
    return pl.pallas_call(
        kernel,
        out_shape=out,
        in_specs=[VMEM] * len(operands),
        out_specs=jax.tree.map(lambda _: VMEM, out),
        scratch_shapes=rest.get("scratch", ()),
        input_output_aliases=rest.get("aliases", {}),
        cost_estimate=pl.CostEstimate(
            flops=rest.get("flops", 0), bytes_accessed=1 << 20, transcendentals=0
        ),
        compiler_params=pltpu.CompilerParams(vmem_limit_bytes=48 << 20),
    )(*operands)


def meet(unit, blocks, total, fresh):
    features = unit.shape[1]
    lands = jnp.concatenate([unit_rows(block[:, :features]) for block in blocks], axis=0)
    vectors = jnp.concatenate([block[:, features:] for block in blocks], axis=0)
    vectors = jnp.concatenate([vectors, jnp.ones_like(vectors)], axis=1)
    for start in range(0, unit.shape[0], TILE):
        rows = slice(start, start + TILE)
        cosine = lax.dot_general(
            unit[rows, :], lands, (((1,), (1,)), ((), ())), preferred_element_type=F32
        )
        kernel = jnp.exp(2.0 * kernel_gain * (cosine - 1.0)).astype(BF16)
        more = jnp.dot(kernel, vectors, preferred_element_type=F32)
        total[rows, :] = more if fresh else total[rows, :] + more


def first_kernel(points, block, unit, total):
    for start in range(0, points.shape[0], TILE):
        rows = slice(start, start + TILE)
        unit[rows, :] = unit_rows(points[rows, :])
    meet(unit, [block], total, True)


def next_kernel(count, unit, *refs):
    blocks, before, total = refs[:count], refs[count], refs[count + 1]
    total[...] = before[...]
    meet(unit, blocks, total, False)


def compact(total, begin, half, out):
    out[:half, :] = total[pl.ds(begin, half), :LANES]
    diagonal = eye(LANES)
    lines = []
    for block in range(half // LANES):
        wide = total[pl.ds(begin + block * LANES, LANES), LANES:]
        lines.append(jnp.sum(jnp.where(diagonal, wide, 0.0), axis=0, keepdims=True))
    lines += [jnp.ones_like(lines[0])] * (-len(lines) % 8)
    out[half:, :] = jnp.concatenate(lines, axis=0)


def last_kernel(count, unit, *refs):
    blocks, before, keep, send, total = refs[:count], *refs[count:]
    total[...] = before[...]
    meet(unit, blocks, total, False)
    half = unit.shape[0] // 2
    core = lax.rem(lax.axis_index("lmk"), 2)
    compact(total, pl.multiple_of(core * half, half), half, keep)
    compact(total, pl.multiple_of(half - core * half, half), half, send)


def pack(value, half, out):
    out[:half, :] = value[:half, :].astype(BF16)
    tail = value[half:, :]
    parts = [part for part in split3(tail)]
    parts.append(jnp.zeros_like(parts[0]))
    out[half:, :] = jnp.concatenate([part.astype(F32) for part in parts], axis=0).astype(BF16)


def unpack(packed, half):
    value = packed[...].astype(F32)
    some = (value.shape[0] - half) // 4
    tail = value[half:, :]
    degree = (tail[2 * some : 3 * some] + tail[some : 2 * some]) + tail[:some]
    return value[:half], degree


def pack_kernel(half, mine, other, out):
    pack(mine[...] + other[...], half, out)


def repack_kernel(half, mine, other, out):
    value, degree = unpack(mine, half)
    more, plus = unpack(other, half)
    pack(jnp.concatenate([value + more, degree + plus], axis=0), half, out)


def gram_kernel(half, mine, other, embed, gram):
    value, degree = unpack(mine, half)
    more, plus = unpack(other, half)
    projected = value + more
    scale = lax.rsqrt(degree + plus)
    diagonal = eye(LANES)
    for block in range(half // LANES):
        rows = slice(block * LANES, (block + 1) * LANES)
        line = jnp.broadcast_to(scale[block : block + 1, :], (LANES, LANES))
        column = jnp.sum(jnp.where(diagonal, line, 0.0), axis=1, keepdims=True)
        embed[rows, :] = projected[rows, :] * column
    gram[...] = lax.dot_general(
        embed[...],
        embed[...],
        (((0,), (0,)), ((), ())),
        precision=lax.Precision.HIGHEST,
        preferred_element_type=F32,
    )


def eliminate(work, rows):
    size = work.shape[0]
    for start in range(0, size, PANEL):
        lines = [
            jnp.broadcast_to(work[start + i : start + i + 1, :], (8, 2 * size))
            for i in range(PANEL)
        ]
        block = {
            (i, k): jnp.broadcast_to(lines[i][:, start + k : start + k + 1], (8, size))
            for i in range(PANEL)
            for k in range(i, PANEL)
        }
        for j in range(PANEL):
            scale = lax.rsqrt(block[j, j])
            line = lines[j] * jnp.concatenate([scale, scale], axis=1)
            rows[start + j : start + j + 1, :] = line[:1]
            times = {i: block[j, i] * scale for i in range(j + 1, PANEL)}
            for i in range(j + 1, PANEL):
                lines[i] = lines[i] - jnp.concatenate([times[i], times[i]], axis=1) * line
                for k in range(i, PANEL):
                    block[i, k] = block[i, k] - times[i] * times[k]
        after = start + PANEL
        if after < size:
            high, mid, low = split3(rows[start:after, :])
            left = jnp.concatenate([high, high, mid, high, low, mid], axis=0)[:, :size]
            right = jnp.concatenate([high, mid, high, low, high, mid], axis=0)
            update = lax.dot_general(
                left, right, (((0,), (0,)), ((), ())), preferred_element_type=F32
            )
            work[after:, :] = work[after:, :] - update[after:, :]


def finish_kernel(points, mine, other, own, theirs, out, work, rows):
    size = mine.shape[0]
    half = own.shape[0]
    work[:, :size] = (mine[...] + other[...]) / points
    work[:, size:] = jnp.where(eye(size), 1.0, 0.0)
    eliminate(work, rows)
    core = lax.rem(lax.axis_index("lmk"), 2)
    for embed, begin in ((own, core * half), (theirs, half - core * half)):
        out[pl.ds(pl.multiple_of(begin, half), half), :] = lax.dot_general(
            embed[...],
            rows[:, size:],
            (((1,), (1,)), ((), ())),
            precision=lax.Precision.HIGHEST,
            preferred_element_type=F32,
        )


def per_device(points, landmarks, eigvecs):
    num_pts = lax.axis_size("pts")
    num_lmk = lax.axis_size("lmk")
    num_rows, features = points.shape
    size = eigvecs.shape[1]
    half = num_rows // 2
    pts_bits = [1 << b for b in reversed(range(num_pts.bit_length() - 1))]
    lmk_bits = [1 << b for b in range(1, num_lmk.bit_length() - 1)]
    shape = jax.ShapeDtypeStruct

    held = {0: jnp.concatenate([landmarks, eigvecs], axis=1)}
    if num_pts == 8:
        hops = [(0, 4), (0, 1), (0, 2), (4, 2), (4, 1), (1, 2), (6, 1)]
        groups = [(1, 2), (4, 6), (5, 3, 7)]
    else:
        hops = []
        for bit in pts_bits:
            hops += [(mask, bit) for mask in [0] + [m ^ b for m, b in hops]]
        order = [mask ^ bit for mask, bit in hops]
        groups = [order[i : i + 4] for i in range(0, len(order), 4)]
    for mask, bit in hops:
        held[mask ^ bit] = swap(held[mask], "pts", num_pts, bit)

    flops = 2 * num_rows * landmarks.shape[0] * (features + 2 * size)
    unit, total = call_on(
        first_kernel,
        (shape((num_rows, features), BF16), shape((num_rows, 2 * size), F32)),
        (points, held[0]),
        flops=flops,
    )
    for group in groups[:-1]:
        total = call_on(
            functools.partial(next_kernel, len(group)),
            shape((num_rows, 2 * size), F32),
            (unit, *[held[mask] for mask in group], total),
            aliases={len(group) + 1: 0},
            flops=flops * len(group),
        )
    group = groups[-1]
    extra = -(-(half // LANES) // 8) * 8
    keep, send = call_on(
        functools.partial(last_kernel, len(group)),
        (shape((half + extra, size), F32),) * 2,
        (unit, *[held[mask] for mask in group], total),
        scratch=[pltpu.VMEM((num_rows, 2 * size), F32)],
        flops=flops * len(group),
    )
    packed = shape((half + 4 * extra, size), BF16)
    mine = call_on(
        functools.partial(pack_kernel, half), packed, (keep, swap(send, "lmk", num_lmk, 1))
    )
    for bit in lmk_bits[:-1]:
        mine = call_on(
            functools.partial(repack_kernel, half), packed, (mine, swap(mine, "lmk", num_lmk, bit))
        )
    embed, gram = call_on(
        functools.partial(gram_kernel, half),
        (shape((half, size), F32), shape((size, size), F32)),
        (mine, swap(mine, "lmk", num_lmk, lmk_bits[-1])),
    )
    gram = gram + swap(gram, "lmk", num_lmk, 1)
    other = swap(embed, "lmk", num_lmk, 1)
    for bit in pts_bits[:-1]:
        gram = gram + swap(gram, "pts", num_pts, bit)
    return call_on(
        functools.partial(finish_kernel, float(num_rows * num_pts)),
        shape((num_rows, size), F32),
        (gram, swap(gram, "pts", num_pts, pts_bits[-1]), embed, other),
        scratch=[pltpu.VMEM((size, 2 * size), F32)] * 2,
    )


def solution(mesh):
    placed = (P("pts", None), P(("pts", "lmk"), None), P(("pts", "lmk"), None))
    return jax.shard_map(
        per_device, mesh=mesh, in_specs=placed, out_specs=P("pts", None), check_vma=False
    )
```

```python
import functools
import math

import jax
import jax.numpy as jnp
from jax import lax
from jax.experimental import pallas as pl
from jax.experimental.pallas import tpu as pltpu
from jax.sharding import PartitionSpec as P

kernel_gain = 16.0
LANES = 128
TILE = 256
PANEL = 16
VMEM = pl.BlockSpec(memory_space=pltpu.VMEM)
BF16 = jnp.bfloat16
F32 = jnp.float32


def unit_rows(values):
    floats = values.astype(F32)
    factor = lax.rsqrt(jnp.mean(floats * floats, axis=-1, keepdims=True) + 1e-06) / math.sqrt(
        values.shape[-1]
    )
    return (floats * factor).astype(BF16)


def split3(value):
    high = value.astype(BF16)
    rest = value - high.astype(F32)
    mid = rest.astype(BF16)
    low = (rest - mid.astype(F32)).astype(BF16)
    return high, mid, low


def swap(value, axis, size, bit):
    return lax.ppermute(value, axis, [(i, i ^ bit) for i in range(size)])


def eye(size):
    row = lax.broadcasted_iota(jnp.int32, (size, size), 0)
    column = lax.broadcasted_iota(jnp.int32, (size, size), 1)
    return row == column


def call_on(kernel, out, operands, **rest):
    return pl.pallas_call(
        kernel,
        out_shape=out,
        in_specs=[VMEM] * len(operands),
        out_specs=jax.tree.map(lambda _: VMEM, out),
        scratch_shapes=rest.get("scratch", ()),
        input_output_aliases=rest.get("aliases", {}),
        cost_estimate=pl.CostEstimate(
            flops=rest.get("flops", 0), bytes_accessed=1 << 20, transcendentals=0
        ),
        compiler_params=pltpu.CompilerParams(vmem_limit_bytes=48 << 20),
    )(*operands)


def beside_kernel(left, right, out, sems):
    width = left.shape[1]
    copies = [
        pltpu.make_async_copy(left, out.at[:, :width], sems.at[0]),
        pltpu.make_async_copy(right, out.at[:, width:], sems.at[1]),
    ]
    for copy in copies:
        copy.start()
    for copy in copies:
        copy.wait()


def meet(unit, blocks, before, total):
    features = unit.shape[1]
    lands = jnp.concatenate([unit_rows(block[:, :features]) for block in blocks], axis=0)
    vectors = jnp.concatenate([block[:, features:] for block in blocks], axis=0)
    vectors = jnp.concatenate([vectors, jnp.ones_like(vectors)], axis=1)
    for start in range(0, unit.shape[0], TILE):
        rows = slice(start, start + TILE)
        cosine = lax.dot_general(
            unit[rows, :], lands, (((1,), (1,)), ((), ())), preferred_element_type=F32
        )
        kernel = jnp.exp(2.0 * kernel_gain * (cosine - 1.0)).astype(BF16)
        more = jnp.dot(kernel, vectors, preferred_element_type=F32)
        total[rows, :] = more if before is None else before[rows, :] + more


def first_kernel(points, block, unit, total):
    for start in range(0, points.shape[0], TILE):
        rows = slice(start, start + TILE)
        unit[rows, :] = unit_rows(points[rows, :])
    meet(unit, [block], None, total)


def next_kernel(count, unit, *refs):
    blocks, before, total = refs[:count], refs[count], refs[count + 1]
    meet(unit, blocks, before, total)


def compact(total, begin, half, out):
    out[:half, :] = total[pl.ds(begin, half), :LANES]
    diagonal = eye(LANES)
    lines = []
    for block in range(half // LANES):
        wide = total[pl.ds(begin + block * LANES, LANES), LANES:]
        lines.append(jnp.sum(jnp.where(diagonal, wide, 0.0), axis=0, keepdims=True))
    lines += [jnp.ones_like(lines[0])] * (-len(lines) % 8)
    out[half:, :] = jnp.concatenate(lines, axis=0)


def last_kernel(count, unit, *refs):
    blocks, before, keep, send, total = refs[:count], *refs[count:]
    meet(unit, blocks, before, total)
    half = unit.shape[0] // 2
    core = lax.rem(lax.axis_index("lmk"), 2)
    compact(total, pl.multiple_of(core * half, half), half, keep)
    compact(total, pl.multiple_of(half - core * half, half), half, send)


def pack(value, half, out):
    out[:half, :] = value[:half, :].astype(BF16)
    tail = value[half:, :]
    parts = [part for part in split3(tail)]
    parts.append(jnp.zeros_like(parts[0]))
    out[half:, :] = jnp.concatenate([part.astype(F32) for part in parts], axis=0).astype(BF16)


def unpack(packed, half):
    value = packed[...].astype(F32)
    some = (value.shape[0] - half) // 4
    tail = value[half:, :]
    degree = (tail[2 * some : 3 * some] + tail[some : 2 * some]) + tail[:some]
    return value[:half], degree


def pack_kernel(half, mine, other, out):
    pack(mine[...] + other[...], half, out)


def repack_kernel(half, mine, other, out):
    value, degree = unpack(mine, half)
    more, plus = unpack(other, half)
    pack(jnp.concatenate([value + more, degree + plus], axis=0), half, out)


def gram_kernel(half, mine, other, embed, gram):
    value, degree = unpack(mine, half)
    more, plus = unpack(other, half)
    projected = value + more
    scale = lax.rsqrt(degree + plus)
    diagonal = eye(LANES)
    for block in range(half // LANES):
        rows = slice(block * LANES, (block + 1) * LANES)
        line = jnp.broadcast_to(scale[block : block + 1, :], (LANES, LANES))
        column = jnp.sum(jnp.where(diagonal, line, 0.0), axis=1, keepdims=True)
        embed[rows, :] = projected[rows, :] * column
    gram[...] = lax.dot_general(
        embed[...],
        embed[...],
        (((0,), (0,)), ((), ())),
        precision=lax.Precision.HIGHEST,
        preferred_element_type=F32,
    )


def eliminate(work, rows):
    size = work.shape[0]
    for start in range(0, size, PANEL):
        lines = [
            jnp.broadcast_to(work[start + i : start + i + 1, :], (8, 2 * size))
            for i in range(PANEL)
        ]
        block = {
            (i, k): jnp.broadcast_to(lines[i][:, start + k : start + k + 1], (8, size))
            for i in range(PANEL)
            for k in range(i, PANEL)
        }
        for j in range(PANEL):
            scale = lax.rsqrt(block[j, j])
            line = lines[j] * jnp.concatenate([scale, scale], axis=1)
            rows[start + j : start + j + 1, :] = line[:1]
            times = {i: block[j, i] * scale for i in range(j + 1, PANEL)}
            for i in range(j + 1, PANEL):
                lines[i] = lines[i] - jnp.concatenate([times[i], times[i]], axis=1) * line
                for k in range(i, PANEL):
                    block[i, k] = block[i, k] - times[i] * times[k]
        after = start + PANEL
        if after < size:
            high, mid, low = split3(rows[start:after, :])
            left = jnp.concatenate([high, high, mid, high, low, mid], axis=0)[:, :size]
            right = jnp.concatenate([high, mid, high, low, high, mid], axis=0)
            update = lax.dot_general(
                left, right, (((0,), (0,)), ((), ())), preferred_element_type=F32
            )
            work[after:, :] = work[after:, :] - update[after:, :]


def finish_kernel(points, mine, other, own, theirs, out, work, rows):
    size = mine.shape[0]
    half = own.shape[0]
    work[:, :size] = (mine[...] + other[...]) / points
    work[:, size:] = jnp.where(eye(size), 1.0, 0.0)
    eliminate(work, rows)
    core = lax.rem(lax.axis_index("lmk"), 2)
    high, low, _ = split3(rows[:, size:])
    right = jnp.concatenate([high, low, high], axis=1)
    for embed, begin in ((own, core * half), (theirs, half - core * half)):
        high, low, _ = split3(embed[...])
        out[pl.ds(pl.multiple_of(begin, half), half), :] = lax.dot_general(
            jnp.concatenate([high, high, low], axis=1),
            right,
            (((1,), (1,)), ((), ())),
            preferred_element_type=F32,
        )


def per_device(points, landmarks, eigvecs):
    num_pts = lax.axis_size("pts")
    num_lmk = lax.axis_size("lmk")
    num_rows, features = points.shape
    size = eigvecs.shape[1]
    half = num_rows // 2
    pts_bits = [1 << b for b in reversed(range(num_pts.bit_length() - 1))]
    lmk_bits = [1 << b for b in range(1, num_lmk.bit_length() - 1)]
    shape = jax.ShapeDtypeStruct

    held = {
        0: pl.pallas_call(
            beside_kernel,
            out_shape=shape((landmarks.shape[0], features + size), BF16),
            in_specs=[pl.BlockSpec(memory_space=pltpu.HBM)] * 2,
            out_specs=VMEM,
            scratch_shapes=[pltpu.SemaphoreType.DMA((2,))],
        )(landmarks, eigvecs)
    }
    if num_pts == 8:
        rounds = [[(0, 4), (0, 1), (0, 2)], [(4, 2), (4, 1)], [(6, 1), (1, 2)]]
    else:
        rounds, order = [], [0]
        for bit in pts_bits:
            rounds.append([(mask, bit) for mask in order])
            order = order + [mask ^ bit for mask in order]

    flops = 8 * num_rows * landmarks.shape[0] * (features + 2 * size)
    ready, unit, total = [0], None, None
    for hops in rounds:
        for mask, bit in hops:
            held[mask ^ bit] = swap(held[mask], "pts", num_pts, bit)
        if unit is None:
            unit, total = call_on(
                first_kernel,
                (shape((num_rows, features), BF16), shape((num_rows, 2 * size), F32)),
                (points, held[0]),
                flops=flops,
            )
        else:
            total = call_on(
                functools.partial(next_kernel, len(ready)),
                shape((num_rows, 2 * size), F32),
                (unit, *[held[mask] for mask in ready], total),
                aliases={len(ready) + 1: 0},
                flops=flops * len(ready),
            )
        ready = [mask ^ bit for mask, bit in hops]
        if hops is not rounds[-1]:
            held, total = lax.optimization_barrier((held, total))
    group = ready
    extra = -(-(half // LANES) // 8) * 8
    keep, send = call_on(
        functools.partial(last_kernel, len(group)),
        (shape((half + extra, size), F32),) * 2,
        (unit, *[held[mask] for mask in group], total),
        scratch=[pltpu.VMEM((num_rows, 2 * size), F32)],
        flops=flops * len(group),
    )
    packed = shape((half + 4 * extra, size), BF16)
    mine = call_on(
        functools.partial(pack_kernel, half), packed, (keep, swap(send, "lmk", num_lmk, 1))
    )
    for bit in lmk_bits[:-1]:
        mine = call_on(
            functools.partial(repack_kernel, half), packed, (mine, swap(mine, "lmk", num_lmk, bit))
        )
    embed, gram = call_on(
        functools.partial(gram_kernel, half),
        (shape((half, size), F32), shape((size, size), F32)),
        (mine, swap(mine, "lmk", num_lmk, lmk_bits[-1])),
    )
    gram = gram + swap(gram, "lmk", num_lmk, 1)
    other = swap(embed, "lmk", num_lmk, 1)
    for bit in pts_bits[:-1]:
        gram = gram + swap(gram, "pts", num_pts, bit)
    return call_on(
        functools.partial(finish_kernel, float(num_rows * num_pts)),
        shape((num_rows, size), F32),
        (gram, swap(gram, "pts", num_pts, pts_bits[-1]), embed, other),
        scratch=[pltpu.VMEM((size, 2 * size), F32)] * 2,
    )


def solution(mesh):
    placed = (P("pts", None), P(("pts", "lmk"), None), P(("pts", "lmk"), None))
    return jax.shard_map(
        per_device, mesh=mesh, in_specs=placed, out_specs=P("pts", None), check_vma=False
    )
```

```python
import functools
import math

import jax
import jax.numpy as jnp
from jax import lax
from jax.experimental import pallas as pl
from jax.experimental.pallas import tpu as pltpu
from jax.sharding import PartitionSpec as P

kernel_gain = 16.0
LANES = 128
TILE = 512
PANEL = 16
VMEM = pl.BlockSpec(memory_space=pltpu.VMEM)
BF16 = jnp.bfloat16
F32 = jnp.float32


def unit_rows(values):
    floats = values.astype(F32)
    factor = lax.rsqrt(jnp.mean(floats * floats, axis=-1, keepdims=True) + 1e-06) / math.sqrt(
        values.shape[-1]
    )
    return (floats * factor).astype(BF16)


def split3(value):
    high = value.astype(BF16)
    rest = value - high.astype(F32)
    mid = rest.astype(BF16)
    low = (rest - mid.astype(F32)).astype(BF16)
    return high, mid, low


def swap(value, axis, size, bit):
    return lax.ppermute(value, axis, [(i, i ^ bit) for i in range(size)])


def eye(size):
    row = lax.broadcasted_iota(jnp.int32, (size, size), 0)
    column = lax.broadcasted_iota(jnp.int32, (size, size), 1)
    return row == column


def call_on(kernel, out, operands, **rest):
    return pl.pallas_call(
        kernel,
        out_shape=out,
        in_specs=[VMEM] * len(operands),
        out_specs=jax.tree.map(lambda _: VMEM, out),
        scratch_shapes=rest.get("scratch", ()),
        input_output_aliases=rest.get("aliases", {}),
        cost_estimate=pl.CostEstimate(
            flops=rest.get("flops", 0), bytes_accessed=1 << 20, transcendentals=0
        ),
        compiler_params=pltpu.CompilerParams(vmem_limit_bytes=48 << 20),
    )(*operands)


def beside_kernel(left, right, out, sems):
    width = left.shape[1]
    copies = [
        pltpu.make_async_copy(left, out.at[:, :width], sems.at[0]),
        pltpu.make_async_copy(right, out.at[:, width:], sems.at[1]),
    ]
    for copy in copies:
        copy.start()
    for copy in copies:
        copy.wait()


def meet(unit, blocks, before, total, begin=0):
    features = unit.shape[1]
    lands = jnp.concatenate([unit_rows(block[:, :features]) for block in blocks], axis=0)
    vectors = jnp.concatenate([block[:, features:] for block in blocks], axis=0)
    vectors = jnp.concatenate([vectors, jnp.ones_like(vectors)], axis=1)
    lands = lands.T
    for start in range(0, total.shape[0], TILE):
        size = min(TILE, total.shape[0] - start)
        rows = pl.ds(start, size)
        cosine = jnp.dot(
            unit[pl.ds(begin + start, size), :], lands, preferred_element_type=F32
        )
        kernel = jnp.exp(2.0 * kernel_gain * (cosine - 1.0)).astype(BF16)
        more = jnp.dot(kernel, vectors, preferred_element_type=F32)
        if before is not None:
            more = more + before[pl.ds(begin + start, size), :]
        total[rows, :] = more


def first_kernel(points, block, unit, total):
    for start in range(0, points.shape[0], TILE):
        rows = slice(start, start + TILE)
        unit[rows, :] = unit_rows(points[rows, :])
    meet(unit, [block], None, total)


def next_kernel(count, unit, *refs):
    blocks, before, total = refs[:count], refs[count], refs[count + 1]
    meet(unit, blocks, before, total)


def last_kernel(count, mine, unit, *refs):
    blocks, before, out, total = refs[:count], *refs[count:]
    half = total.shape[0]
    core = lax.rem(lax.axis_index("lmk"), 2)
    begin = core * half if mine else half - core * half
    meet(unit, blocks, before, total, pl.multiple_of(begin, half))
    out[:half, :] = total[:, :LANES]
    diagonal = eye(LANES)
    lines = []
    for start in range(0, half, LANES):
        wide = total[start : start + LANES, LANES:]
        lines.append(jnp.sum(jnp.where(diagonal, wide, 0.0), axis=0, keepdims=True))
    lines += [jnp.ones_like(lines[0])] * (-len(lines) % 8)
    out[half:, :] = jnp.concatenate(lines, axis=0)


def pack(value, half, out):
    out[:half, :] = value[:half, :].astype(BF16)
    tail = value[half:, :]
    parts = [part for part in split3(tail)]
    parts.append(jnp.zeros_like(parts[0]))
    out[half:, :] = jnp.concatenate([part.astype(F32) for part in parts], axis=0).astype(BF16)


def unpack(packed, half):
    value = packed[...].astype(F32)
    some = (value.shape[0] - half) // 4
    tail = value[half:, :]
    degree = (tail[2 * some : 3 * some] + tail[some : 2 * some]) + tail[:some]
    return value[:half], degree


def pack_kernel(half, mine, other, out):
    pack(mine[...] + other[...], half, out)


def repack_kernel(half, mine, other, out):
    value, degree = unpack(mine, half)
    more, plus = unpack(other, half)
    pack(jnp.concatenate([value + more, degree + plus], axis=0), half, out)


def gram_kernel(half, mine, other, embed, gram):
    value, degree = unpack(mine, half)
    more, plus = unpack(other, half)
    projected = value + more
    scale = lax.rsqrt(degree + plus)
    diagonal = eye(LANES)
    for block in range(half // LANES):
        rows = slice(block * LANES, (block + 1) * LANES)
        line = jnp.broadcast_to(scale[block : block + 1, :], (LANES, LANES))
        column = jnp.sum(jnp.where(diagonal, line, 0.0), axis=1, keepdims=True)
        embed[rows, :] = projected[rows, :] * column
    gram[...] = lax.dot_general(
        embed[...],
        embed[...],
        (((0,), (0,)), ((), ())),
        precision=lax.Precision.HIGHEST,
        preferred_element_type=F32,
    )


def eliminate(work, rows):
    size = work.shape[0]
    for start in range(0, size, PANEL):
        lines = [
            jnp.broadcast_to(work[start + i : start + i + 1, :], (8, 2 * size))
            for i in range(PANEL)
        ]
        block = {
            (i, k): jnp.broadcast_to(lines[i][:, start + k : start + k + 1], (8, size))
            for i in range(PANEL)
            for k in range(i, PANEL)
        }
        for j in range(PANEL):
            scale = lax.rsqrt(block[j, j])
            line = lines[j] * jnp.concatenate([scale, scale], axis=1)
            rows[start + j : start + j + 1, :] = line[:1]
            times = {i: block[j, i] * scale for i in range(j + 1, PANEL)}
            for i in range(j + 1, PANEL):
                lines[i] = lines[i] - jnp.concatenate([times[i], times[i]], axis=1) * line
                for k in range(i, PANEL):
                    block[i, k] = block[i, k] - times[i] * times[k]
        after = start + PANEL
        if after < size:
            high, mid, low = split3(rows[start:after, :])
            left = jnp.concatenate([high, high, mid, high, low, mid], axis=0)[:, :size]
            right = jnp.concatenate([high, mid, high, low, high, mid], axis=0)
            update = lax.dot_general(
                left, right, (((0,), (0,)), ((), ())), preferred_element_type=F32
            )
            work[after:, :] = work[after:, :] - update[after:, :]


def finish_kernel(points, gram, own, theirs, out, work, rows):
    size = gram.shape[0]
    half = own.shape[0]
    work[:, :size] = gram[...] / points
    work[:, size:] = jnp.where(eye(size), 1.0, 0.0)
    eliminate(work, rows)
    core = lax.rem(lax.axis_index("lmk"), 2)
    high, low, _ = split3(rows[:, size:])
    right = jnp.concatenate([high, low, high], axis=1)
    for embed, begin in ((own, core * half), (theirs, half - core * half)):
        high, low, _ = split3(embed[...])
        out[pl.ds(pl.multiple_of(begin, half), half), :] = lax.dot_general(
            jnp.concatenate([high, high, low], axis=1),
            right,
            (((1,), (1,)), ((), ())),
            preferred_element_type=F32,
        )


def per_device(points, landmarks, eigvecs):
    num_pts = lax.axis_size("pts")
    num_lmk = lax.axis_size("lmk")
    num_rows, features = points.shape
    size = eigvecs.shape[1]
    half = num_rows // 2
    pts_bits = [1 << b for b in reversed(range(num_pts.bit_length() - 1))]
    lmk_bits = [1 << b for b in range(1, num_lmk.bit_length() - 1)]
    shape = jax.ShapeDtypeStruct

    held = {
        0: pl.pallas_call(
            beside_kernel,
            out_shape=shape((landmarks.shape[0], features + size), BF16),
            in_specs=[pl.BlockSpec(memory_space=pltpu.HBM)] * 2,
            out_specs=VMEM,
            scratch_shapes=[pltpu.SemaphoreType.DMA((2,))],
        )(landmarks, eigvecs)
    }
    if num_pts == 8:
        rounds = [[(0, 4), (0, 1), (0, 2)], [(4, 2), (4, 1)], [(6, 1), (1, 2)]]
    else:
        rounds, order = [], [0]
        for bit in pts_bits:
            rounds.append([(mask, bit) for mask in order])
            order = order + [mask ^ bit for mask in order]

    flops = 8 * num_rows * landmarks.shape[0] * (features + 2 * size)
    ready, unit, total = [0], None, None
    for turn, hops in enumerate(rounds):
        for mask, bit in hops:
            held[mask ^ bit] = swap(held[mask], "pts", num_pts, bit)
        if unit is None:
            unit, total = call_on(
                first_kernel,
                (shape((num_rows, features), BF16), shape((num_rows, 2 * size), F32)),
                (points, held[0]),
                flops=flops,
            )
        else:
            total = call_on(
                functools.partial(next_kernel, len(ready)),
                shape((num_rows, 2 * size), F32),
                (unit, *[held[mask] for mask in ready], total),
                aliases={len(ready) + 1: 0},
                flops=flops * len(ready),
            )
        ready = [mask ^ bit for mask, bit in hops]
        if turn + 1 < len(rounds):
            tied = list(dict.fromkeys([mask for mask, _ in rounds[turn + 1]] + ready))
            *fresh, total = lax.optimization_barrier((*[held[mask] for mask in tied], total))
            held.update(zip(tied, fresh))
    group = ready
    extra = -(-(half // LANES) // 8) * 8
    send, keep = [
        call_on(
            functools.partial(last_kernel, len(group), mine),
            shape((half + extra, size), F32),
            (unit, *[held[mask] for mask in group], total),
            scratch=[pltpu.VMEM((half, 2 * size), F32)],
            flops=flops * len(group) // 2,
        )
        for mine in (False, True)
    ]
    packed = shape((half + 4 * extra, size), BF16)
    mine = call_on(
        functools.partial(pack_kernel, half), packed, (keep, swap(send, "lmk", num_lmk, 1))
    )
    for bit in lmk_bits[:-1]:
        mine = call_on(
            functools.partial(repack_kernel, half), packed, (mine, swap(mine, "lmk", num_lmk, bit))
        )
    embed, gram = call_on(
        functools.partial(gram_kernel, half),
        (shape((half, size), F32), shape((size, size), F32)),
        (mine, swap(mine, "lmk", num_lmk, lmk_bits[-1])),
    )
    gram = gram + swap(gram, "lmk", num_lmk, 1)
    other = swap(embed, "lmk", num_lmk, 1)
    pieces = gram.reshape(num_pts, size // num_pts, size)
    pieces = jnp.sum(lax.all_to_all(pieces, "pts", 0, 0, tiled=False), axis=0)
    pieces = jnp.broadcast_to(pieces, (num_pts, *pieces.shape))
    gram = lax.all_to_all(pieces, "pts", 0, 0, tiled=False).reshape(size, size)
    return call_on(
        functools.partial(finish_kernel, float(num_rows * num_pts)),
        shape((num_rows, size), F32),
        (gram, embed, other),
        scratch=[pltpu.VMEM((size, 2 * size), F32)] * 2,
    )


def solution(mesh):
    placed = (P("pts", None), P(("pts", "lmk"), None), P(("pts", "lmk"), None))
    return jax.shard_map(
        per_device, mesh=mesh, in_specs=placed, out_specs=P("pts", None), check_vma=False
    )
```

```python
import functools
import math

import jax
import jax.numpy as jnp
from jax import lax
from jax.experimental import pallas as pl
from jax.experimental.pallas import tpu as pltpu
from jax.sharding import PartitionSpec as P

kernel_gain = 16.0
LANES = 128
TILE = 512
PANEL = 16
SUB = 8
VMEM = pl.BlockSpec(memory_space=pltpu.VMEM)
BF16 = jnp.bfloat16
F32 = jnp.float32


def unit_rows(values):
    floats = values.astype(F32)
    factor = lax.rsqrt(jnp.mean(floats * floats, axis=-1, keepdims=True) + 1e-06) / math.sqrt(
        values.shape[-1]
    )
    return (floats * factor).astype(BF16)


def split3(value):
    high = value.astype(BF16)
    rest = value - high.astype(F32)
    mid = rest.astype(BF16)
    low = (rest - mid.astype(F32)).astype(BF16)
    return high, mid, low


def swap(value, axis, size, bit):
    return lax.ppermute(value, axis, [(i, i ^ bit) for i in range(size)])


def eye(size):
    row = lax.broadcasted_iota(jnp.int32, (size, size), 0)
    column = lax.broadcasted_iota(jnp.int32, (size, size), 1)
    return row == column


def call_on(kernel, out, operands, **rest):
    return pl.pallas_call(
        kernel,
        out_shape=out,
        in_specs=[VMEM] * len(operands),
        out_specs=jax.tree.map(lambda _: VMEM, out),
        scratch_shapes=rest.get("scratch", ()),
        input_output_aliases=rest.get("aliases", {}),
        cost_estimate=pl.CostEstimate(
            flops=rest.get("flops", 0), bytes_accessed=1 << 20, transcendentals=0
        ),
        compiler_params=pltpu.CompilerParams(vmem_limit_bytes=48 << 20),
    )(*operands)


def beside_kernel(left, right, out):
    out[:, : left.shape[1]] = left[...]
    out[:, left.shape[1] :] = right[...]


def meet(unit, blocks, before, total, begin=0):
    features = unit.shape[1]
    lands = jnp.concatenate([unit_rows(block[:, :features]) for block in blocks], axis=0)
    vectors = jnp.concatenate([block[:, features:] for block in blocks], axis=0)
    vectors = jnp.concatenate([vectors, jnp.ones_like(vectors)], axis=1)
    lands = lands.T
    for start in range(0, total.shape[0], TILE):
        size = min(TILE, total.shape[0] - start)
        rows = pl.ds(start, size)
        cosine = jnp.dot(
            unit[pl.ds(begin + start, size), :], lands, preferred_element_type=F32
        )
        kernel = jnp.exp(2.0 * kernel_gain * (cosine - 1.0)).astype(BF16)
        more = jnp.dot(kernel, vectors, preferred_element_type=F32)
        if before is not None:
            more = more + before[pl.ds(begin + start, size), :]
        total[rows, :] = more


def first_kernel(points, block, unit, total):
    for start in range(0, points.shape[0], TILE):
        rows = slice(start, start + TILE)
        unit[rows, :] = unit_rows(points[rows, :])
    meet(unit, [block], None, total)


def next_kernel(count, unit, *refs):
    blocks, before, total = refs[:count], refs[count], refs[count + 1]
    meet(unit, blocks, before, total)


def last_kernel(count, mine, unit, *refs):
    blocks, before, out, total = refs[:count], *refs[count:]
    half = total.shape[0]
    core = lax.rem(lax.axis_index("lmk"), 2)
    begin = core * half if mine else half - core * half
    meet(unit, blocks, before, total, pl.multiple_of(begin, half))
    out[:half, :] = total[:, :LANES]
    diagonal = eye(LANES)
    lines = []
    for start in range(0, half, LANES):
        wide = total[start : start + LANES, LANES:]
        lines.append(jnp.sum(jnp.where(diagonal, wide, 0.0), axis=0, keepdims=True))
    lines += [jnp.ones_like(lines[0])] * (-len(lines) % 8)
    out[half:, :] = jnp.concatenate(lines, axis=0)


def pack(value, half, out):
    out[:half, :] = value[:half, :].astype(BF16)
    tail = value[half:, :]
    parts = [part for part in split3(tail)]
    parts.append(jnp.zeros_like(parts[0]))
    out[half:, :] = jnp.concatenate([part.astype(F32) for part in parts], axis=0).astype(BF16)


def unpack(packed, half):
    value = packed[...].astype(F32)
    some = (value.shape[0] - half) // 4
    tail = value[half:, :]
    degree = (tail[2 * some : 3 * some] + tail[some : 2 * some]) + tail[:some]
    return value[:half], degree


def pack_kernel(half, mine, other, out):
    pack(mine[...] + other[...], half, out)


def repack_kernel(half, mine, other, out):
    value, degree = unpack(mine, half)
    more, plus = unpack(other, half)
    pack(jnp.concatenate([value + more, degree + plus], axis=0), half, out)


def gram_kernel(half, mine, other, embed, keep, send, gram):
    value, degree = unpack(mine, half)
    more, plus = unpack(other, half)
    projected = value + more
    scale = lax.rsqrt(degree + plus)
    diagonal = eye(LANES)
    for block in range(half // LANES):
        rows = slice(block * LANES, (block + 1) * LANES)
        line = jnp.broadcast_to(scale[block : block + 1, :], (LANES, LANES))
        column = jnp.sum(jnp.where(diagonal, line, 0.0), axis=1, keepdims=True)
        embed[rows, :] = projected[rows, :] * column
    gram[...] = lax.dot_general(
        embed[...],
        embed[...],
        (((0,), (0,)), ((), ())),
        precision=lax.Precision.HIGHEST,
        preferred_element_type=F32,
    )
    some = keep.shape[0]
    begin = lax.rem(lax.axis_index("lmk"), 2) * some
    keep[...] = gram[pl.ds(pl.multiple_of(begin, some), some), :]
    send[...] = gram[pl.ds(pl.multiple_of(some - begin, some), some), :]


def parts_kernel(own, theirs, out):
    half = own.shape[0]
    core = lax.rem(lax.axis_index("lmk"), 2)
    for embed, begin in ((own, core * half), (theirs, half - core * half)):
        high, low, _ = split3(embed[...])
        out[pl.ds(pl.multiple_of(begin, half), half), :] = jnp.concatenate(
            [high, high, low], axis=1
        )


def eliminate(work, rows):
    size = work.shape[0]
    for start in range(0, size, PANEL):
        lines = [
            jnp.broadcast_to(work[start + i : start + i + 1, :], (8, 2 * size))
            for i in range(PANEL)
        ]

        def lane(i, k):
            return jnp.broadcast_to(lines[i][:, start + k : start + k + 1], (8, size))

        for sub in range(0, PANEL, SUB):
            inside = range(sub, sub + SUB)
            block = {(i, k): lane(i, k) for i in inside for k in range(i, sub + SUB)}
            for j in inside:
                scale = lax.rsqrt(block[j, j])
                lines[j] = lines[j] * jnp.concatenate([scale, scale], axis=1)
                rows[start + j : start + j + 1, :] = lines[j][:1]
                times = {
                    i: block[j, i] * scale if i in inside else lane(j, i)
                    for i in range(j + 1, PANEL)
                }
                for i, factor in times.items():
                    lines[i] = lines[i] - jnp.concatenate([factor, factor], axis=1) * lines[j]
                    if i in inside:
                        for k in range(i, sub + SUB):
                            block[i, k] = block[i, k] - factor * times[k]
        after = start + PANEL
        if after < size:
            high, mid, low = split3(rows[start:after, :])
            left = jnp.concatenate([high, high, mid, high, low, mid], axis=0)[:, :size]
            right = jnp.concatenate([high, mid, high, low, high, mid], axis=0)
            update = lax.dot_general(
                left, right, (((0,), (0,)), ((), ())), preferred_element_type=F32
            )
            work[after:, :] = work[after:, :] - update[after:, :]


def finish_kernel(points, own, theirs, parts, out, work, rows):
    some, size = own.shape
    begin = lax.rem(lax.axis_index("lmk"), 2) * some
    work[pl.ds(pl.multiple_of(begin, some), some), :size] = own[...] / points
    work[pl.ds(pl.multiple_of(some - begin, some), some), :size] = theirs[...] / points
    work[:, size:] = jnp.where(eye(size), 1.0, 0.0)
    eliminate(work, rows)
    high, low, _ = split3(rows[:, size:])
    out[...] = lax.dot_general(
        parts[...],
        jnp.concatenate([high, low, high], axis=1),
        (((1,), (1,)), ((), ())),
        preferred_element_type=F32,
    )


def per_device(points, landmarks, eigvecs):
    num_pts = lax.axis_size("pts")
    num_lmk = lax.axis_size("lmk")
    num_rows, features = points.shape
    size = eigvecs.shape[1]
    half = num_rows // 2
    pts_bits = [1 << b for b in reversed(range(num_pts.bit_length() - 1))]
    lmk_bits = [1 << b for b in range(1, num_lmk.bit_length() - 1)]
    shape = jax.ShapeDtypeStruct

    held = {
        0: call_on(
            beside_kernel,
            shape((landmarks.shape[0], features + size), BF16),
            (landmarks, eigvecs),
        )
    }
    if num_pts == 8:
        rounds = [[(0, 4), (0, 2), (0, 1)], [(4, 2), (4, 1)], [(6, 1)]]
        late = (1, 2)
    else:
        rounds, order, late = [], [0], None
        for bit in pts_bits:
            rounds.append([(mask, bit) for mask in order])
            order = order + [mask ^ bit for mask in order]

    flops = 8 * num_rows * landmarks.shape[0] * (features + 2 * size)
    ready, unit, total = [0], None, None
    for turn, hops in enumerate(rounds):
        for mask, bit in hops:
            held[mask ^ bit] = swap(held[mask], "pts", num_pts, bit)
        if unit is None:
            unit, total = call_on(
                first_kernel,
                (shape((num_rows, features), BF16), shape((num_rows, 2 * size), F32)),
                (points, held[0]),
                flops=flops,
            )
        else:
            total = call_on(
                functools.partial(next_kernel, len(ready)),
                shape((num_rows, 2 * size), F32),
                (unit, *[held[mask] for mask in ready], total),
                aliases={len(ready) + 1: 0},
                flops=flops * len(ready),
            )
        ready = [mask ^ bit for mask, bit in hops]
        if turn == 1 and late:
            mask, bit = late
            held[mask], total = lax.optimization_barrier((held[mask], total))
            held[mask ^ bit] = swap(held[mask], "pts", num_pts, bit)
        if turn + 1 < len(rounds):
            tied = list(dict.fromkeys(ready + [mask for mask, _ in rounds[turn + 1]]))[::-1]
            *fresh, total = lax.optimization_barrier((*[held[mask] for mask in tied], total))
            held.update(zip(tied, fresh))
    group = ready + ([late[0] ^ late[1]] if late else [])
    extra = -(-(half // LANES) // 8) * 8
    send, keep = [
        call_on(
            functools.partial(last_kernel, len(group), mine),
            shape((half + extra, size), F32),
            (unit, *[held[mask] for mask in group], total),
            scratch=[pltpu.VMEM((half, 2 * size), F32)],
            flops=flops * len(group) // 2,
        )
        for mine in (False, True)
    ]
    packed = shape((half + 4 * extra, size), BF16)
    mine = call_on(
        functools.partial(pack_kernel, half), packed, (keep, swap(send, "lmk", num_lmk, 1))
    )
    for bit in lmk_bits[:-1]:
        mine = call_on(
            functools.partial(repack_kernel, half), packed, (mine, swap(mine, "lmk", num_lmk, bit))
        )
    embed, part, send = call_on(
        functools.partial(gram_kernel, half),
        (shape((half, size), F32), *[shape((size // 2, size), F32)] * 2),
        (mine, swap(mine, "lmk", num_lmk, lmk_bits[-1])),
        scratch=[pltpu.VMEM((size, size), F32)],
    )
    part = part + swap(send, "lmk", num_lmk, 1)
    parts = call_on(
        parts_kernel,
        shape((num_rows, 3 * size), BF16),
        (embed, swap(embed, "lmk", num_lmk, 1)),
    )
    for bit in pts_bits:
        part = part + swap(part, "pts", num_pts, bit)
    return call_on(
        functools.partial(finish_kernel, float(num_rows * num_pts)),
        shape((num_rows, size), F32),
        (part, swap(part, "lmk", num_lmk, 1), parts),
        scratch=[pltpu.VMEM((size, 2 * size), F32)] * 2,
    )


def solution(mesh):
    placed = (P("pts", None), P(("pts", "lmk"), None), P(("pts", "lmk"), None))
    return jax.shard_map(
        per_device, mesh=mesh, in_specs=placed, out_specs=P("pts", None), check_vma=False
    )
```

```python
import functools
import math

import jax
import jax.numpy as jnp
from jax import lax
from jax.experimental import pallas as pl
from jax.experimental.pallas import tpu as pltpu
from jax.sharding import PartitionSpec as P

kernel_gain = 16.0
LANES = 128
TILE = 512
PANEL = 8
VMEM = pl.BlockSpec(memory_space=pltpu.VMEM)
BF16 = jnp.bfloat16
F32 = jnp.float32


def unit_rows(values):
    floats = values.astype(F32)
    factor = lax.rsqrt(jnp.mean(floats * floats, axis=-1, keepdims=True) + 1e-06) / math.sqrt(
        values.shape[-1]
    )
    return (floats * factor).astype(BF16)


def split3(value):
    high = value.astype(BF16)
    rest = value - high.astype(F32)
    mid = rest.astype(BF16)
    low = (rest - mid.astype(F32)).astype(BF16)
    return high, mid, low


def swap(value, axis, size, bit):
    return lax.ppermute(value, axis, [(i, i ^ bit) for i in range(size)])


def eye(size):
    row = lax.broadcasted_iota(jnp.int32, (size, size), 0)
    column = lax.broadcasted_iota(jnp.int32, (size, size), 1)
    return row == column


def call_on(kernel, out, operands, **rest):
    return pl.pallas_call(
        kernel,
        out_shape=out,
        in_specs=[rest.get("in_specs", VMEM)] * len(operands),
        out_specs=rest.get("out_specs", jax.tree.map(lambda _: VMEM, out)),
        scratch_shapes=rest.get("scratch", ()),
        input_output_aliases=rest.get("aliases", {}),
        cost_estimate=pl.CostEstimate(
            flops=rest.get("flops", 0), bytes_accessed=1 << 20, transcendentals=0
        ),
        compiler_params=pltpu.CompilerParams(vmem_limit_bytes=48 << 20),
    )(*operands)


def beside_kernel(left, right, out, sems):
    width = left.shape[1]
    copies = [pltpu.make_async_copy(right, out.at[:, width:], sems.at[0])]
    for start in range(0, left.shape[0], 16):
        rows = pl.ds(start, 16)
        copies.append(
            pltpu.make_async_copy(left.at[rows], out.at[rows, :width], sems.at[len(copies)])
        )
    for copy in copies:
        copy.start()
    for copy in copies:
        copy.wait()


def meet(unit, blocks, before, total, begin=0):
    features = unit.shape[1]
    lands = jnp.concatenate([unit_rows(block[:, :features]) for block in blocks], axis=0)
    vectors = jnp.concatenate([block[:, features:] for block in blocks], axis=0)
    vectors = jnp.concatenate([vectors, jnp.ones_like(vectors)], axis=1)
    lands = lands.T
    for start in range(0, total.shape[0], TILE):
        size = min(TILE, total.shape[0] - start)
        rows = pl.ds(start, size)
        cosine = jnp.dot(
            unit[pl.ds(begin + start, size), :], lands, preferred_element_type=F32
        )
        kernel = jnp.exp(2.0 * kernel_gain * (cosine - 1.0)).astype(BF16)
        more = jnp.dot(kernel, vectors, preferred_element_type=F32)
        if before is not None:
            more = more + before[pl.ds(begin + start, size), :]
        total[rows, :] = more


def first_kernel(points, block, unit, total):
    for start in range(0, points.shape[0], TILE):
        rows = slice(start, start + TILE)
        unit[rows, :] = unit_rows(points[rows, :])
    meet(unit, [block], None, total)


def next_kernel(count, unit, *refs):
    blocks, before, total = refs[:count], refs[count], refs[count + 1]
    meet(unit, blocks, before, total)


def last_kernel(count, mine, unit, *refs):
    blocks, before, out, total = refs[:count], *refs[count:]
    half = total.shape[0]
    core = lax.rem(lax.axis_index("lmk"), 2)
    begin = core * half if mine else half - core * half
    meet(unit, blocks, before, total, pl.multiple_of(begin, half))
    out[:half, :] = total[:, :LANES]
    diagonal = eye(LANES)
    lines = []
    for start in range(0, half, LANES):
        wide = total[start : start + LANES, LANES:]
        lines.append(jnp.sum(jnp.where(diagonal, wide, 0.0), axis=0, keepdims=True))
    lines += [jnp.ones_like(lines[0])] * (-len(lines) % 8)
    out[half:, :] = jnp.concatenate(lines, axis=0)


def pack(value, half, out):
    out[:half, :] = value[:half, :].astype(BF16)
    tail = value[half:, :]
    parts = [part for part in split3(tail)]
    parts.append(jnp.zeros_like(parts[0]))
    out[half:, :] = jnp.concatenate([part.astype(F32) for part in parts], axis=0).astype(BF16)


def unpack(packed, half):
    value = packed[...].astype(F32)
    some = (value.shape[0] - half) // 4
    tail = value[half:, :]
    degree = (tail[2 * some : 3 * some] + tail[some : 2 * some]) + tail[:some]
    return value[:half], degree


def pack_kernel(half, mine, other, out):
    pack(mine[...] + other[...], half, out)


def repack_kernel(half, mine, other, out):
    value, degree = unpack(mine, half)
    more, plus = unpack(other, half)
    pack(jnp.concatenate([value + more, degree + plus], axis=0), half, out)


def gram_kernel(half, mine, other, embed, keep, send, gram):
    value, degree = unpack(mine, half)
    more, plus = unpack(other, half)
    projected = value + more
    scale = lax.rsqrt(degree + plus)
    diagonal = eye(LANES)
    for block in range(half // LANES):
        rows = slice(block * LANES, (block + 1) * LANES)
        line = jnp.broadcast_to(scale[block : block + 1, :], (LANES, LANES))
        column = jnp.sum(jnp.where(diagonal, line, 0.0), axis=1, keepdims=True)
        embed[rows, :] = projected[rows, :] * column
    gram[...] = lax.dot_general(
        embed[...],
        embed[...],
        (((0,), (0,)), ((), ())),
        precision=lax.Precision.HIGHEST,
        preferred_element_type=F32,
    )
    some = keep.shape[0]
    begin = lax.rem(lax.axis_index("lmk"), 2) * some
    keep[...] = gram[pl.ds(pl.multiple_of(begin, some), some), :]
    send[...] = gram[pl.ds(pl.multiple_of(some - begin, some), some), :]


def parts_kernel(own, theirs, out):
    half = own.shape[0]
    core = lax.rem(lax.axis_index("lmk"), 2)
    for embed, begin in ((own, core * half), (theirs, half - core * half)):
        high, low, _ = split3(embed[...])
        out[pl.ds(pl.multiple_of(begin, half), half), :] = jnp.concatenate(
            [high, high, low], axis=1
        )


def eliminate(work, rows):
    size = work.shape[0]

    def load(start):
        return [
            jnp.broadcast_to(work[start + i : start + i + 1, :], (8, 2 * size))
            for i in range(PANEL)
        ]

    def twice(value):
        return jnp.concatenate([value, value], axis=1)

    lines = load(0)
    for start in range(0, size, PANEL):
        ahead = load(start + PANEL) if start + PANEL < size else []

        def lane(i, k):
            return jnp.broadcast_to(lines[i][:, start + k : start + k + 1], (8, size))

        block = {(i, k): lane(i, k) for i in range(PANEL) for k in range(i, PANEL)}
        for j in range(PANEL):
            scale = lax.rsqrt(block[j, j])
            lines[j] = lines[j] * twice(scale)
            rows[start + j : start + j + 1, :] = lines[j][:1]
            times = {i: block[j, i] * scale for i in range(j + 1, PANEL)}
            for i, factor in times.items():
                lines[i] = lines[i] - twice(factor) * lines[j]
                for k in range(i, PANEL):
                    block[i, k] = block[i, k] - factor * times[k]
            for i in range(len(ahead)):
                ahead[i] = ahead[i] - twice(lane(j, PANEL + i)) * lines[j]
        behind = start + 2 * PANEL
        if behind < size:
            high, mid, low = [
                part.astype(F32) for part in split3(rows[start : start + PANEL, :])
            ]
            left = jnp.concatenate([high, high, mid, high, low, mid], axis=0)[:, :size]
            right = jnp.concatenate([high, mid, high, low, high, mid], axis=0)
            update = lax.dot_general(
                left.astype(BF16),
                right.astype(BF16),
                (((0,), (0,)), ((), ())),
                preferred_element_type=F32,
            )
            work[behind:, :] = work[behind:, :] - update[behind:, :]
        lines = ahead


def finish_kernel(points, own, theirs, parts, out, work, rows, result, sems):
    some, size = own.shape
    begin = lax.rem(lax.axis_index("lmk"), 2) * some
    work[pl.ds(pl.multiple_of(begin, some), some), :size] = own[...] / points
    work[pl.ds(pl.multiple_of(some - begin, some), some), :size] = theirs[...] / points
    work[:, size:] = jnp.where(eye(size), 1.0, 0.0)
    eliminate(work, rows)
    high, low, _ = split3(rows[:, size:])
    right = jnp.concatenate([high, low, high], axis=1)
    copies = []
    for start in range(0, parts.shape[0], TILE):
        lines = pl.ds(start, min(TILE, parts.shape[0] - start))
        result[lines, :] = lax.dot_general(
            parts[lines, :], right, (((1,), (1,)), ((), ())), preferred_element_type=F32
        )
        copies.append(
            pltpu.make_async_copy(result.at[lines], out.at[lines], sems.at[len(copies)])
        )
        copies[-1].start()
    for copy in copies:
        copy.wait()


def per_device(points, landmarks, eigvecs):
    num_pts = lax.axis_size("pts")
    num_lmk = lax.axis_size("lmk")
    num_rows, features = points.shape
    size = eigvecs.shape[1]
    half = num_rows // 2
    pts_bits = [1 << b for b in reversed(range(num_pts.bit_length() - 1))]
    lmk_bits = [1 << b for b in range(1, num_lmk.bit_length() - 1)]
    shape = jax.ShapeDtypeStruct

    held = {
        0: call_on(
            beside_kernel,
            shape((landmarks.shape[0], features + size), BF16),
            (landmarks, eigvecs),
            scratch=[pltpu.SemaphoreType.DMA((1 + landmarks.shape[0] // 16,))],
            in_specs=pl.BlockSpec(memory_space=pltpu.HBM),
        )
    }
    if num_pts == 8:
        rounds = [[(0, 4), (0, 2), (0, 1)], [(4, 2), (4, 1)], [(6, 1)]]
        late = (1, 2)
    else:
        rounds, order, late = [], [0], None
        for bit in pts_bits:
            rounds.append([(mask, bit) for mask in order])
            order = order + [mask ^ bit for mask in order]

    flops = 8 * num_rows * landmarks.shape[0] * (features + 2 * size)
    ready, unit, total = [0], None, None
    for turn, hops in enumerate(rounds):
        for mask, bit in hops:
            held[mask ^ bit] = swap(held[mask], "pts", num_pts, bit)
        if unit is None:
            unit, total = call_on(
                first_kernel,
                (shape((num_rows, features), BF16), shape((num_rows, 2 * size), F32)),
                (points, held[0]),
                flops=flops,
            )
        else:
            total = call_on(
                functools.partial(next_kernel, len(ready)),
                shape((num_rows, 2 * size), F32),
                (unit, *[held[mask] for mask in ready], total),
                aliases={len(ready) + 1: 0},
                flops=flops * len(ready),
            )
        ready = [mask ^ bit for mask, bit in hops]
        if turn == 1 and late:
            mask, bit = late
            held[mask], total = lax.optimization_barrier((held[mask], total))
            held[mask ^ bit] = swap(held[mask], "pts", num_pts, bit)
        if turn + 1 < len(rounds):
            tied = list(dict.fromkeys(ready + [mask for mask, _ in rounds[turn + 1]]))[::-1]
            *fresh, total = lax.optimization_barrier((*[held[mask] for mask in tied], total))
            held.update(zip(tied, fresh))
    group = ready + ([late[0] ^ late[1]] if late else [])
    extra = -(-(half // LANES) // 8) * 8
    send, keep = [
        call_on(
            functools.partial(last_kernel, len(group), mine),
            shape((half + extra, size), F32),
            (unit, *[held[mask] for mask in group], total),
            scratch=[pltpu.VMEM((half, 2 * size), F32)],
            flops=flops * len(group) // 2,
        )
        for mine in (False, True)
    ]
    packed = shape((half + 4 * extra, size), BF16)
    mine = call_on(
        functools.partial(pack_kernel, half), packed, (keep, swap(send, "lmk", num_lmk, 1))
    )
    for bit in lmk_bits[:-1]:
        mine = call_on(
            functools.partial(repack_kernel, half), packed, (mine, swap(mine, "lmk", num_lmk, bit))
        )
    embed, part, send = call_on(
        functools.partial(gram_kernel, half),
        (shape((half, size), F32), *[shape((size // 2, size), F32)] * 2),
        (mine, swap(mine, "lmk", num_lmk, lmk_bits[-1])),
        scratch=[pltpu.VMEM((size, size), F32)],
    )
    part = part + swap(send, "lmk", num_lmk, 1)
    parts = call_on(
        parts_kernel,
        shape((num_rows, 3 * size), BF16),
        (embed, swap(embed, "lmk", num_lmk, 1)),
    )
    part = lax.psum(part, "pts")
    return call_on(
        functools.partial(finish_kernel, float(num_rows * num_pts)),
        shape((num_rows, size), F32),
        (part, swap(part, "lmk", num_lmk, 1), parts),
        scratch=[
            *[pltpu.VMEM((size, 2 * size), F32)] * 2,
            pltpu.VMEM((num_rows, size), F32),
            pltpu.SemaphoreType.DMA((-(-num_rows // TILE),)),
        ],
        out_specs=pl.BlockSpec(memory_space=pltpu.HBM),
    )


def solution(mesh):
    placed = (P("pts", None), P(("pts", "lmk"), None), P(("pts", "lmk"), None))
    return jax.shard_map(
        per_device, mesh=mesh, in_specs=placed, out_specs=P("pts", None), check_vma=False
    )
```

```python
import functools
import math

import jax
import jax.numpy as jnp
from jax import lax
from jax.experimental import pallas as pl
from jax.experimental.pallas import tpu as pltpu
from jax.sharding import PartitionSpec as P

kernel_gain = 16.0
LANES = 128
TILE = 512
PANEL = 8
VMEM = pl.BlockSpec(memory_space=pltpu.VMEM)
BF16 = jnp.bfloat16
F32 = jnp.float32


def unit_rows(values):
    floats = values.astype(F32)
    factor = lax.rsqrt(jnp.mean(floats * floats, axis=-1, keepdims=True) + 1e-06) / math.sqrt(
        values.shape[-1]
    )
    return (floats * factor).astype(BF16)


def split3(value):
    high = value.astype(BF16)
    rest = value - high.astype(F32)
    mid = rest.astype(BF16)
    low = (rest - mid.astype(F32)).astype(BF16)
    return high, mid, low


def swap(value, axis, size, bit):
    return lax.ppermute(value, axis, [(i, i ^ bit) for i in range(size)])


def eye(size):
    row = lax.broadcasted_iota(jnp.int32, (size, size), 0)
    column = lax.broadcasted_iota(jnp.int32, (size, size), 1)
    return row == column


def call_on(kernel, out, operands, **rest):
    return pl.pallas_call(
        kernel,
        out_shape=out,
        in_specs=[rest.get("in_specs", VMEM)] * len(operands),
        out_specs=rest.get("out_specs", jax.tree.map(lambda _: VMEM, out)),
        scratch_shapes=rest.get("scratch", ()),
        input_output_aliases=rest.get("aliases", {}),
        cost_estimate=pl.CostEstimate(
            flops=rest.get("flops", 0), bytes_accessed=1 << 20, transcendentals=0
        ),
        compiler_params=pltpu.CompilerParams(vmem_limit_bytes=48 << 20),
    )(*operands)


def beside_kernel(left, right, out, sems):
    width = left.shape[1]
    copies = [pltpu.make_async_copy(right, out.at[:, width:], sems.at[0])]
    for start in range(0, left.shape[0], 16):
        rows = pl.ds(start, 16)
        copies.append(
            pltpu.make_async_copy(left.at[rows], out.at[rows, :width], sems.at[len(copies)])
        )
    for copy in copies:
        copy.start()
    for copy in copies:
        copy.wait()


def meet(unit, blocks, before, total, begin=0):
    features = unit.shape[1]
    lands = jnp.concatenate([unit_rows(block[:, :features]) for block in blocks], axis=0)
    vectors = jnp.concatenate([block[:, features:] for block in blocks], axis=0)
    vectors = jnp.concatenate([vectors, jnp.ones_like(vectors)], axis=1)
    lands = lands.T
    for start in range(0, total.shape[0], TILE):
        size = min(TILE, total.shape[0] - start)
        rows = pl.ds(start, size)
        cosine = jnp.dot(
            unit[pl.ds(begin + start, size), :], lands, preferred_element_type=F32
        )
        kernel = jnp.exp(2.0 * kernel_gain * (cosine - 1.0)).astype(BF16)
        more = jnp.dot(kernel, vectors, preferred_element_type=F32)
        if before is not None:
            more = more + before[pl.ds(begin + start, size), :]
        total[rows, :] = more


def first_kernel(points, block, unit, total):
    for start in range(0, points.shape[0], TILE):
        rows = slice(start, start + TILE)
        unit[rows, :] = unit_rows(points[rows, :])
    meet(unit, [block], None, total)


def next_kernel(count, unit, *refs):
    blocks, before, total = refs[:count], refs[count], refs[count + 1]
    meet(unit, blocks, before, total)


def last_kernel(count, mine, unit, *refs):
    blocks, before, out, total = refs[:count], *refs[count:]
    half = total.shape[0]
    core = lax.rem(lax.axis_index("lmk"), 2)
    begin = core * half if mine else half - core * half
    meet(unit, blocks, before, total, pl.multiple_of(begin, half))
    out[:half, :] = total[:, :LANES]
    diagonal = eye(LANES)
    lines = []
    for start in range(0, half, LANES):
        wide = total[start : start + LANES, LANES:]
        lines.append(jnp.sum(jnp.where(diagonal, wide, 0.0), axis=0, keepdims=True))
    lines += [jnp.ones_like(lines[0])] * (-len(lines) % 8)
    out[half:, :] = jnp.concatenate(lines, axis=0)


def pack(value, half, out):
    out[:half, :] = value[:half, :].astype(BF16)
    tail = value[half:, :]
    parts = [part for part in split3(tail)]
    parts.append(jnp.zeros_like(parts[0]))
    out[half:, :] = jnp.concatenate([part.astype(F32) for part in parts], axis=0).astype(BF16)


def unpack(packed, half):
    value = packed[...].astype(F32)
    some = (value.shape[0] - half) // 4
    tail = value[half:, :]
    degree = (tail[2 * some : 3 * some] + tail[some : 2 * some]) + tail[:some]
    return value[:half], degree


def pack_kernel(half, mine, other, out):
    pack(mine[...] + other[...], half, out)


def repack_kernel(half, mine, other, out):
    value, degree = unpack(mine, half)
    more, plus = unpack(other, half)
    pack(jnp.concatenate([value + more, degree + plus], axis=0), half, out)


def gram_kernel(half, mine, other, embed, keep, send, gram):
    value, degree = unpack(mine, half)
    more, plus = unpack(other, half)
    projected = value + more
    scale = lax.rsqrt(degree + plus)
    diagonal = eye(LANES)
    for block in range(half // LANES):
        rows = slice(block * LANES, (block + 1) * LANES)
        line = jnp.broadcast_to(scale[block : block + 1, :], (LANES, LANES))
        column = jnp.sum(jnp.where(diagonal, line, 0.0), axis=1, keepdims=True)
        embed[rows, :] = projected[rows, :] * column
    gram[...] = lax.dot_general(
        embed[...],
        embed[...],
        (((0,), (0,)), ((), ())),
        precision=lax.Precision.HIGHEST,
        preferred_element_type=F32,
    )
    some = keep.shape[0]
    begin = lax.rem(lax.axis_index("lmk"), 2) * some
    keep[...] = gram[pl.ds(pl.multiple_of(begin, some), some), :]
    send[...] = gram[pl.ds(pl.multiple_of(some - begin, some), some), :]


def parts_kernel(own, theirs, out):
    half = own.shape[0]
    core = lax.rem(lax.axis_index("lmk"), 2)
    for embed, begin in ((own, core * half), (theirs, half - core * half)):
        high, low, _ = split3(embed[...])
        out[pl.ds(pl.multiple_of(begin, half), half), :] = jnp.concatenate(
            [high, high, low], axis=1
        )


def eliminate(work, rows):
    size = work.shape[0]

    def load(start):
        return [
            jnp.broadcast_to(work[start + i : start + i + 1, :], (8, 2 * size))
            for i in range(PANEL)
        ]

    def twice(value):
        return jnp.concatenate([value, value], axis=1)

    lines = load(0)
    for start in range(0, size, PANEL):
        ahead = load(start + PANEL) if start + PANEL < size else []

        def lane(i, k):
            return jnp.broadcast_to(lines[i][:, start + k : start + k + 1], (8, size))

        block = {(i, k): lane(i, k) for i in range(PANEL) for k in range(i, PANEL)}
        for j in range(PANEL):
            scale = lax.rsqrt(block[j, j])
            lines[j] = lines[j] * twice(scale)
            rows[start + j : start + j + 1, :] = lines[j][:1]
            times = {i: block[j, i] * scale for i in range(j + 1, PANEL)}
            for i, factor in times.items():
                lines[i] = lines[i] - twice(factor) * lines[j]
                for k in range(i, PANEL):
                    block[i, k] = block[i, k] - factor * times[k]
            for i in range(len(ahead)):
                ahead[i] = ahead[i] - twice(lane(j, PANEL + i)) * lines[j]
        behind = start + 2 * PANEL
        if behind < size:
            high, mid, low = [
                part.astype(F32) for part in split3(rows[start : start + PANEL, :])
            ]
            left = jnp.concatenate([high, high, mid, high, low, mid], axis=0)[:, :size]
            right = jnp.concatenate([high, mid, high, low, high, mid], axis=0)
            update = lax.dot_general(
                left.astype(BF16),
                right.astype(BF16),
                (((0,), (0,)), ((), ())),
                preferred_element_type=F32,
            )
            work[behind:, :] = work[behind:, :] - update[behind:, :]
        lines = ahead


def finish_kernel(points, own, theirs, parts, out, work, rows, result, sems):
    some, size = own.shape
    begin = lax.rem(lax.axis_index("lmk"), 2) * some
    work[pl.ds(pl.multiple_of(begin, some), some), :size] = own[...] / points
    work[pl.ds(pl.multiple_of(some - begin, some), some), :size] = theirs[...] / points
    work[:, size:] = jnp.where(eye(size), 1.0, 0.0)
    eliminate(work, rows)
    high, low, _ = split3(rows[:, size:])
    right = jnp.concatenate([high, low, high], axis=1)
    copies = []
    for start in range(0, parts.shape[0], TILE):
        lines = pl.ds(start, min(TILE, parts.shape[0] - start))
        result[lines, :] = lax.dot_general(
            parts[lines, :], right, (((1,), (1,)), ((), ())), preferred_element_type=F32
        )
        copies.append(
            pltpu.make_async_copy(result.at[lines], out.at[lines], sems.at[len(copies)])
        )
        copies[-1].start()
    for copy in copies:
        copy.wait()


def per_device(points, landmarks, eigvecs):
    num_pts = lax.axis_size("pts")
    num_lmk = lax.axis_size("lmk")
    num_rows, features = points.shape
    size = eigvecs.shape[1]
    half = num_rows // 2
    pts_bits = [1 << b for b in reversed(range(num_pts.bit_length() - 1))]
    lmk_bits = [1 << b for b in range(1, num_lmk.bit_length() - 1)]
    shape = jax.ShapeDtypeStruct

    held = {
        0: pl.pallas_call(
            beside_kernel,
            out_shape=shape((landmarks.shape[0], features + size), BF16),
            in_specs=[pl.BlockSpec(memory_space=pltpu.HBM)] * 2,
            out_specs=VMEM,
            scratch_shapes=[pltpu.SemaphoreType.DMA((1 + landmarks.shape[0] // 16,))],
        )(landmarks, eigvecs)
    }
    if num_pts == 8:
        rounds = [[(0, 4), (0, 2), (0, 1)], [(4, 2), (4, 1)], [(6, 1)]]
        late = (1, 2)
    else:
        rounds, order, late = [], [0], None
        for bit in pts_bits:
            rounds.append([(mask, bit) for mask in order])
            order = order + [mask ^ bit for mask in order]

    flops = 8 * num_rows * landmarks.shape[0] * (features + 2 * size)

    def more(total, masks):
        return call_on(
            functools.partial(next_kernel, len(masks)),
            shape((num_rows, 2 * size), F32),
            (unit, *[held[mask] for mask in masks], total),
            aliases={len(masks) + 1: 0},
            flops=flops * len(masks),
        )

    ready, unit, total = [0], None, None
    for turn, hops in enumerate(rounds):
        for mask, bit in hops:
            held[mask ^ bit] = swap(held[mask], "pts", num_pts, bit)
        if unit is None:
            unit, total = call_on(
                first_kernel,
                (shape((num_rows, features), BF16), shape((num_rows, 2 * size), F32)),
                (points, held[0]),
                flops=flops,
            )
        else:
            total = more(total, ready)
        ready = [mask ^ bit for mask, bit in hops]
        if turn == 1 and late:
            mask, bit = late
            held[mask], total = lax.optimization_barrier((held[mask], total))
            held[mask ^ bit] = swap(held[mask], "pts", num_pts, bit)
        if turn + 1 < len(rounds):
            sources = [mask for mask, _ in rounds[turn + 1]]
            tied = list(dict.fromkeys(ready + sources))[::-1]
            *fresh, total = lax.optimization_barrier((*[held[mask] for mask in tied], total))
            held.update(zip(tied, fresh))
    if late:
        total = more(total, [late[0] ^ late[1]])
    group = ready
    extra = -(-(half // LANES) // 8) * 8
    send, keep = [
        call_on(
            functools.partial(last_kernel, len(group), mine),
            shape((half + extra, size), F32),
            (unit, *[held[mask] for mask in group], total),
            scratch=[pltpu.VMEM((half, 2 * size), F32)],
            flops=flops * len(group) // 2,
        )
        for mine in (False, True)
    ]
    packed = shape((half + 4 * extra, size), BF16)
    mine = call_on(
        functools.partial(pack_kernel, half), packed, (keep, swap(send, "lmk", num_lmk, 1))
    )
    for bit in lmk_bits[:-1]:
        mine = call_on(
            functools.partial(repack_kernel, half), packed, (mine, swap(mine, "lmk", num_lmk, bit))
        )
    embed, part, send = call_on(
        functools.partial(gram_kernel, half),
        (shape((half, size), F32), *[shape((size // 2, size), F32)] * 2),
        (mine, swap(mine, "lmk", num_lmk, lmk_bits[-1])),
        scratch=[pltpu.VMEM((size, size), F32)],
    )
    part = part + swap(send, "lmk", num_lmk, 1)
    parts = call_on(
        parts_kernel,
        shape((num_rows, 3 * size), BF16),
        (embed, swap(embed, "lmk", num_lmk, 1)),
    )
    if num_pts == 8:
        pair = part + swap(part, "pts", num_pts, 1)
        part = pair + (swap(part, "pts", num_pts, 2) + swap(part, "pts", num_pts, 3))
        pts_bits = [4]
    for bit in pts_bits:
        part = part + swap(part, "pts", num_pts, bit)
    return call_on(
        functools.partial(finish_kernel, float(num_rows * num_pts)),
        shape((num_rows, size), F32),
        (part, swap(part, "lmk", num_lmk, 1), parts),
        scratch=[
            *[pltpu.VMEM((size, 2 * size), F32)] * 2,
            pltpu.VMEM((num_rows, size), F32),
            pltpu.SemaphoreType.DMA((-(-num_rows // TILE),)),
        ],
        out_specs=pl.BlockSpec(memory_space=pltpu.HBM),
    )


def solution(mesh):
    placed = (P("pts", None), P(("pts", "lmk"), None), P(("pts", "lmk"), None))
    return jax.shard_map(
        per_device, mesh=mesh, in_specs=placed, out_specs=P("pts", None), check_vma=False
    )
```

```python
import functools
import math

import jax
import jax.numpy as jnp
from jax import lax
from jax.experimental import pallas as pl
from jax.experimental.pallas import tpu as pltpu
from jax.sharding import PartitionSpec as P

kernel_gain = 16.0
LANES = 128
TILE = 512
PANEL = 16
VMEM = pl.BlockSpec(memory_space=pltpu.VMEM)
BF16 = jnp.bfloat16
F32 = jnp.float32


def unit_rows(values):
    floats = values.astype(F32)
    factor = lax.rsqrt(jnp.mean(floats * floats, axis=-1, keepdims=True) + 1e-06) / math.sqrt(
        values.shape[-1]
    )
    return (floats * factor).astype(BF16)


def split3(value):
    high = value.astype(BF16)
    rest = value - high.astype(F32)
    mid = rest.astype(BF16)
    low = (rest - mid.astype(F32)).astype(BF16)
    return high, mid, low


def swap(value, axis, size, bit):
    return lax.ppermute(value, axis, [(i, i ^ bit) for i in range(size)])


def eye(size):
    row = lax.broadcasted_iota(jnp.int32, (size, size), 0)
    column = lax.broadcasted_iota(jnp.int32, (size, size), 1)
    return row == column


def call_on(kernel, out, operands, **rest):
    return pl.pallas_call(
        kernel,
        out_shape=out,
        in_specs=[rest.get("in_specs", VMEM)] * len(operands),
        out_specs=rest.get("out_specs", jax.tree.map(lambda _: VMEM, out)),
        scratch_shapes=rest.get("scratch", ()),
        input_output_aliases=rest.get("aliases", {}),
        cost_estimate=pl.CostEstimate(
            flops=rest.get("flops", 0), bytes_accessed=1 << 20, transcendentals=0
        ),
        compiler_params=pltpu.CompilerParams(vmem_limit_bytes=48 << 20),
    )(*operands)


def join_kernel(left, right, out):
    out[:, : left.shape[1]] = left[...]
    out[:, left.shape[1] :] = right[...]


def beside_kernel(left, right, out, sems):
    width = left.shape[1]
    copies = [pltpu.make_async_copy(right, out.at[:, width:], sems.at[0])]
    for start in range(0, left.shape[0], 16):
        rows = pl.ds(start, 16)
        copies.append(
            pltpu.make_async_copy(left.at[rows], out.at[rows, :width], sems.at[len(copies)])
        )
    for copy in copies:
        copy.start()
    for copy in copies:
        copy.wait()


def meet(unit, blocks, before, total, begin=0):
    features = unit.shape[1]
    lands = jnp.concatenate([unit_rows(block[:, :features]) for block in blocks], axis=0)
    vectors = jnp.concatenate([block[:, features:] for block in blocks], axis=0)
    vectors = jnp.concatenate([vectors, jnp.ones_like(vectors)], axis=1)
    lands = lands.T
    for start in range(0, total.shape[0], TILE):
        size = min(TILE, total.shape[0] - start)
        rows = pl.ds(start, size)
        cosine = jnp.dot(
            unit[pl.ds(begin + start, size), :], lands, preferred_element_type=F32
        )
        kernel = jnp.exp(2.0 * kernel_gain * (cosine - 1.0)).astype(BF16)
        more = jnp.dot(kernel, vectors, preferred_element_type=F32)
        if before is not None:
            more = more + before[pl.ds(begin + start, size), :]
        total[rows, :] = more


def first_kernel(points, block, unit, total):
    for start in range(0, points.shape[0], TILE):
        rows = slice(start, start + TILE)
        unit[rows, :] = unit_rows(points[rows, :])
    meet(unit, [block], None, total)


def next_kernel(count, unit, *refs):
    blocks, before, total = refs[:count], refs[count], refs[count + 1]
    meet(unit, blocks, before, total)


def last_kernel(count, mine, unit, *refs):
    blocks, before, out, total = refs[:count], *refs[count:]
    half = total.shape[0]
    core = lax.rem(lax.axis_index("lmk"), 2)
    begin = core * half if mine else half - core * half
    meet(unit, blocks, before, total, pl.multiple_of(begin, half))
    out[:half, :] = total[:, :LANES]
    diagonal = eye(LANES)
    lines = []
    for start in range(0, half, LANES):
        wide = total[start : start + LANES, LANES:]
        lines.append(jnp.sum(jnp.where(diagonal, wide, 0.0), axis=0, keepdims=True))
    lines += [jnp.ones_like(lines[0])] * (-len(lines) % 8)
    out[half:, :] = jnp.concatenate(lines, axis=0)


def pack(value, half, out):
    out[:half, :] = value[:half, :].astype(BF16)
    tail = value[half:, :]
    parts = [part for part in split3(tail)]
    parts.append(jnp.zeros_like(parts[0]))
    out[half:, :] = jnp.concatenate([part.astype(F32) for part in parts], axis=0).astype(BF16)


def unpack(packed, half):
    value = packed[...].astype(F32)
    some = (value.shape[0] - half) // 4
    tail = value[half:, :]
    degree = (tail[2 * some : 3 * some] + tail[some : 2 * some]) + tail[:some]
    return value[:half], degree


def pack_kernel(half, mine, other, out):
    pack(mine[...] + other[...], half, out)


def repack_kernel(half, mine, other, out):
    value, degree = unpack(mine, half)
    more, plus = unpack(other, half)
    pack(jnp.concatenate([value + more, degree + plus], axis=0), half, out)


def gram_kernel(half, mine, other, embed, keep, send, gram):
    value, degree = unpack(mine, half)
    more, plus = unpack(other, half)
    projected = value + more
    scale = lax.rsqrt(degree + plus)
    diagonal = eye(LANES)
    for block in range(half // LANES):
        rows = slice(block * LANES, (block + 1) * LANES)
        line = jnp.broadcast_to(scale[block : block + 1, :], (LANES, LANES))
        column = jnp.sum(jnp.where(diagonal, line, 0.0), axis=1, keepdims=True)
        embed[rows, :] = projected[rows, :] * column
    gram[...] = lax.dot_general(
        embed[...],
        embed[...],
        (((0,), (0,)), ((), ())),
        precision=lax.Precision.HIGHEST,
        preferred_element_type=F32,
    )
    some = keep.shape[0]
    begin = lax.rem(lax.axis_index("lmk"), 2) * some
    keep[...] = gram[pl.ds(pl.multiple_of(begin, some), some), :]
    send[...] = gram[pl.ds(pl.multiple_of(some - begin, some), some), :]


def parts_kernel(own, theirs, out):
    half = own.shape[0]
    core = lax.rem(lax.axis_index("lmk"), 2)
    for embed, begin in ((own, core * half), (theirs, half - core * half)):
        high, low, _ = split3(embed[...])
        out[pl.ds(pl.multiple_of(begin, half), half), :] = jnp.concatenate(
            [high, high, low], axis=1
        )


def eliminate(work, rows):
    size = work.shape[0]

    def load(start):
        return [
            jnp.broadcast_to(work[start + i : start + i + 1, :], (8, 2 * size))
            for i in range(PANEL)
        ]

    def twice(value):
        return jnp.concatenate([value, value], axis=1)

    lines = load(0)
    for start in range(0, size, PANEL):
        ahead = load(start + PANEL) if start + PANEL < size else []

        def lane(i, k):
            return jnp.broadcast_to(lines[i][:, start + k : start + k + 1], (8, size))

        block = {(i, k): lane(i, k) for i in range(PANEL) for k in range(i, PANEL)}
        for j in range(PANEL):
            scale = lax.rsqrt(block[j, j])
            lines[j] = lines[j] * twice(scale)
            rows[start + j : start + j + 1, :] = lines[j][:1]
            times = {i: block[j, i] * scale for i in range(j + 1, PANEL)}
            for i, factor in times.items():
                lines[i] = lines[i] - twice(factor) * lines[j]
                for k in range(i, PANEL):
                    block[i, k] = block[i, k] - factor * times[k]
            for i in range(len(ahead)):
                ahead[i] = ahead[i] - twice(lane(j, PANEL + i)) * lines[j]
        behind = start + 2 * PANEL
        if behind < size:
            high, mid, low = [
                part.astype(F32) for part in split3(rows[start : start + PANEL, :])
            ]
            left = jnp.concatenate([high, high, mid, high, low, mid], axis=0)[:, :size]
            right = jnp.concatenate([high, mid, high, low, high, mid], axis=0)
            update = lax.dot_general(
                left.astype(BF16),
                right.astype(BF16),
                (((0,), (0,)), ((), ())),
                preferred_element_type=F32,
            )
            work[behind:, :] = work[behind:, :] - update[behind:, :]
        lines = ahead


def finish_kernel(points, own, theirs, parts, out, work, rows, result, sems):
    some, size = own.shape
    begin = lax.rem(lax.axis_index("lmk"), 2) * some
    work[pl.ds(pl.multiple_of(begin, some), some), :size] = own[...] / points
    work[pl.ds(pl.multiple_of(some - begin, some), some), :size] = theirs[...] / points
    work[:, size:] = jnp.where(eye(size), 1.0, 0.0)
    eliminate(work, rows)
    high, low, _ = split3(rows[:, size:])
    right = jnp.concatenate([high, low, high], axis=1)
    copies = []
    for start in range(0, parts.shape[0], TILE):
        lines = pl.ds(start, min(TILE, parts.shape[0] - start))
        result[lines, :] = lax.dot_general(
            parts[lines, :], right, (((1,), (1,)), ((), ())), preferred_element_type=F32
        )
        copies.append(
            pltpu.make_async_copy(result.at[lines], out.at[lines], sems.at[len(copies)])
        )
        copies[-1].start()
    for copy in copies:
        copy.wait()


def per_device(points, landmarks, eigvecs):
    num_pts = lax.axis_size("pts")
    num_lmk = lax.axis_size("lmk")
    num_rows, features = points.shape
    size = eigvecs.shape[1]
    half = num_rows // 2
    pts_bits = [1 << b for b in reversed(range(num_pts.bit_length() - 1))]
    lmk_bits = [1 << b for b in range(1, num_lmk.bit_length() - 1)]
    shape = jax.ShapeDtypeStruct

    own = (landmarks, eigvecs)
    joined = shape((landmarks.shape[0], features + size), BF16)
    held = {}
    if num_pts == 8:
        held[4] = [swap(value, "pts", num_pts, 4) for value in own]
    held[0] = pl.pallas_call(
        beside_kernel,
        out_shape=joined,
        in_specs=[pl.BlockSpec(memory_space=pltpu.HBM)] * 2,
        out_specs=VMEM,
        scratch_shapes=[pltpu.SemaphoreType.DMA((1 + landmarks.shape[0] // 16,))],
    )(*own)
    if num_pts == 8:
        rounds = [[(0, 4), (0, 2), (0, 1)], [(4, 2), (4, 1)], [(6, 1)]]
        late = (1, 2)
    else:
        rounds, order, late = [], [0], None
        for bit in pts_bits:
            rounds.append([(mask, bit) for mask in order])
            order = order + [mask ^ bit for mask in order]

    flops = 8 * num_rows * landmarks.shape[0] * (features + 2 * size)

    def more(total, masks):
        return call_on(
            functools.partial(next_kernel, len(masks)),
            shape((num_rows, 2 * size), F32),
            (unit, *[held[mask] for mask in masks], total),
            aliases={len(masks) + 1: 0},
            flops=flops * len(masks),
        )

    ready, unit, total = [0], None, None
    for turn, hops in enumerate(rounds):
        for mask, bit in hops:
            if mask ^ bit in held:
                continue
            held[mask ^ bit] = swap(held[mask], "pts", num_pts, bit)
        if unit is None:
            unit, total = call_on(
                first_kernel,
                (shape((num_rows, features), BF16), shape((num_rows, 2 * size), F32)),
                (points, held[0]),
                flops=flops * 4,
            )
        else:
            total = more(total, ready)
        ready = [mask ^ bit for mask, bit in hops]
        if turn == 1 and late:
            mask, bit = late
            held[mask], total = lax.optimization_barrier((held[mask], total))
            held[mask ^ bit] = swap(held[mask], "pts", num_pts, bit)
        if turn + 1 < len(rounds):
            sources = [mask for mask, _ in rounds[turn + 1]]
            tied = list(dict.fromkeys(ready + sources))[::-1]
            *fresh, total = lax.optimization_barrier((*[held[mask] for mask in tied], total))
            held.update(zip(tied, fresh))
            if turn == 0 and late:
                held[4] = call_on(join_kernel, joined, held[4])
    if late:
        total = more(total, [late[0] ^ late[1]])
    group = ready
    extra = -(-(half // LANES) // 8) * 8
    send, keep = [
        call_on(
            functools.partial(last_kernel, len(group), mine),
            shape((half + extra, size), F32),
            (unit, *[held[mask] for mask in group], total),
            scratch=[pltpu.VMEM((half, 2 * size), F32)],
            flops=flops * len(group) // 2,
        )
        for mine in (False, True)
    ]
    packed = shape((half + 4 * extra, size), BF16)
    mine = call_on(
        functools.partial(pack_kernel, half), packed, (keep, swap(send, "lmk", num_lmk, 1))
    )
    for bit in lmk_bits[:-1]:
        mine = call_on(
            functools.partial(repack_kernel, half), packed, (mine, swap(mine, "lmk", num_lmk, bit))
        )
    embed, part, send = call_on(
        functools.partial(gram_kernel, half),
        (shape((half, size), F32), *[shape((size // 2, size), F32)] * 2),
        (mine, swap(mine, "lmk", num_lmk, lmk_bits[-1])),
        scratch=[pltpu.VMEM((size, size), F32)],
    )
    part = part + swap(send, "lmk", num_lmk, 1)
    parts = call_on(
        parts_kernel,
        shape((num_rows, 3 * size), BF16),
        (embed, swap(embed, "lmk", num_lmk, 1)),
    )
    if num_pts == 8:
        pair = part + swap(part, "pts", num_pts, 1)
        part = pair + (swap(part, "pts", num_pts, 2) + swap(part, "pts", num_pts, 3))
        pts_bits = [4]
    for bit in pts_bits:
        part = part + swap(part, "pts", num_pts, bit)
    return call_on(
        functools.partial(finish_kernel, float(num_rows * num_pts)),
        shape((num_rows, size), F32),
        (part, swap(part, "lmk", num_lmk, 1), parts),
        scratch=[
            *[pltpu.VMEM((size, 2 * size), F32)] * 2,
            pltpu.VMEM((num_rows, size), F32),
            pltpu.SemaphoreType.DMA((-(-num_rows // TILE),)),
        ],
        out_specs=pl.BlockSpec(memory_space=pltpu.HBM),
    )


def solution(mesh):
    placed = (P("pts", None), P(("pts", "lmk"), None), P(("pts", "lmk"), None))
    return jax.shard_map(
        per_device, mesh=mesh, in_specs=placed, out_specs=P("pts", None), check_vma=False
    )
```

```python
import functools
import math

import jax
import jax.numpy as jnp
from jax import lax
from jax.experimental import pallas as pl
from jax.experimental.pallas import tpu as pltpu
from jax.sharding import PartitionSpec as P

kernel_gain = 16.0
LANES = 128
TILE = 512
PANEL = 8
VMEM = pl.BlockSpec(memory_space=pltpu.VMEM)
BF16 = jnp.bfloat16
F32 = jnp.float32


def unit_rows(values):
    floats = values.astype(F32)
    factor = lax.rsqrt(jnp.mean(floats * floats, axis=-1, keepdims=True) + 1e-06) / math.sqrt(
        values.shape[-1]
    )
    return (floats * factor).astype(BF16)


def split3(value):
    high = value.astype(BF16)
    rest = value - high.astype(F32)
    mid = rest.astype(BF16)
    low = (rest - mid.astype(F32)).astype(BF16)
    return high, mid, low


def swap(value, axis, size, bit):
    return lax.ppermute(value, axis, [(i, i ^ bit) for i in range(size)])


def eye(size):
    row = lax.broadcasted_iota(jnp.int32, (size, size), 0)
    column = lax.broadcasted_iota(jnp.int32, (size, size), 1)
    return row == column


def call_on(kernel, out, operands, **rest):
    return pl.pallas_call(
        kernel,
        out_shape=out,
        in_specs=[rest.get("in_specs", VMEM)] * len(operands),
        out_specs=rest.get("out_specs", jax.tree.map(lambda _: VMEM, out)),
        scratch_shapes=rest.get("scratch", ()),
        input_output_aliases=rest.get("aliases", {}),
        cost_estimate=pl.CostEstimate(
            flops=rest.get("flops", 0), bytes_accessed=1 << 20, transcendentals=0
        ),
        compiler_params=pltpu.CompilerParams(vmem_limit_bytes=48 << 20),
    )(*operands)


def join_kernel(left, right, out):
    out[:, : left.shape[1]] = left[...]
    out[:, left.shape[1] :] = right[...]


def beside_kernel(left, right, out, sems):
    width = left.shape[1]
    copies = [pltpu.make_async_copy(right, out.at[:, width:], sems.at[0])]
    for start in range(0, left.shape[0], 16):
        rows = pl.ds(start, 16)
        copies.append(
            pltpu.make_async_copy(left.at[rows], out.at[rows, :width], sems.at[len(copies)])
        )
    for copy in copies:
        copy.start()
    for copy in copies:
        copy.wait()


def meet(unit, blocks, before, total, begin=0):
    features = unit.shape[1]
    lands = jnp.concatenate([unit_rows(block[:, :features]) for block in blocks], axis=0)
    vectors = jnp.concatenate([block[:, features:] for block in blocks], axis=0)
    vectors = jnp.concatenate([vectors, jnp.ones_like(vectors)], axis=1)
    lands = lands.T
    for start in range(0, total.shape[0], TILE):
        size = min(TILE, total.shape[0] - start)
        rows = pl.ds(start, size)
        cosine = jnp.dot(
            unit[pl.ds(begin + start, size), :], lands, preferred_element_type=F32
        )
        kernel = jnp.exp(2.0 * kernel_gain * (cosine - 1.0)).astype(BF16)
        more = jnp.dot(kernel, vectors, preferred_element_type=F32)
        if before is not None:
            more = more + before[pl.ds(begin + start, size), :]
        total[rows, :] = more


def first_kernel(points, block, unit, total):
    for start in range(0, points.shape[0], TILE):
        rows = slice(start, start + TILE)
        unit[rows, :] = unit_rows(points[rows, :])
    meet(unit, [block], None, total)


def next_kernel(count, unit, *refs):
    blocks, before, total = refs[:count], refs[count], refs[count + 1]
    meet(unit, blocks, before, total)


def last_kernel(count, mine, unit, *refs):
    blocks, before, out, total = refs[:count], *refs[count:]
    half = total.shape[0]
    core = lax.rem(lax.axis_index("lmk"), 2)
    begin = core * half if mine else half - core * half
    meet(unit, blocks, before, total, pl.multiple_of(begin, half))
    out[:half, :] = total[:, :LANES]
    diagonal = eye(LANES)
    lines = []
    for start in range(0, half, LANES):
        wide = total[start : start + LANES, LANES:]
        lines.append(jnp.sum(jnp.where(diagonal, wide, 0.0), axis=0, keepdims=True))
    lines += [jnp.ones_like(lines[0])] * (-len(lines) % 8)
    out[half:, :] = jnp.concatenate(lines, axis=0)


def pack(value, half, out):
    out[:half, :] = value[:half, :].astype(BF16)
    tail = value[half:, :]
    parts = [part for part in split3(tail)]
    parts.append(jnp.zeros_like(parts[0]))
    out[half:, :] = jnp.concatenate([part.astype(F32) for part in parts], axis=0).astype(BF16)


def unpack(packed, half):
    value = packed[...].astype(F32)
    some = (value.shape[0] - half) // 4
    tail = value[half:, :]
    degree = (tail[2 * some : 3 * some] + tail[some : 2 * some]) + tail[:some]
    return value[:half], degree


def pack_kernel(half, mine, other, out):
    pack(mine[...] + other[...], half, out)


def repack_kernel(half, mine, other, out):
    value, degree = unpack(mine, half)
    more, plus = unpack(other, half)
    pack(jnp.concatenate([value + more, degree + plus], axis=0), half, out)


def gram_kernel(half, mine, other, embed, keep, send, gram):
    value, degree = unpack(mine, half)
    more, plus = unpack(other, half)
    projected = value + more
    scale = lax.rsqrt(degree + plus)
    diagonal = eye(LANES)
    for block in range(half // LANES):
        rows = slice(block * LANES, (block + 1) * LANES)
        line = jnp.broadcast_to(scale[block : block + 1, :], (LANES, LANES))
        column = jnp.sum(jnp.where(diagonal, line, 0.0), axis=1, keepdims=True)
        embed[rows, :] = projected[rows, :] * column
    gram[...] = lax.dot_general(
        embed[...],
        embed[...],
        (((0,), (0,)), ((), ())),
        precision=lax.Precision.HIGHEST,
        preferred_element_type=F32,
    )
    some = keep.shape[0]
    begin = lax.rem(lax.axis_index("lmk"), 2) * some
    keep[...] = gram[pl.ds(pl.multiple_of(begin, some), some), :]
    send[...] = gram[pl.ds(pl.multiple_of(some - begin, some), some), :]


def parts_kernel(own, theirs, out):
    half = own.shape[0]
    core = lax.rem(lax.axis_index("lmk"), 2)
    for embed, begin in ((own, core * half), (theirs, half - core * half)):
        high, low, _ = split3(embed[...])
        out[pl.ds(pl.multiple_of(begin, half), half), :] = jnp.concatenate(
            [high, high, low], axis=1
        )


def eliminate(work, rows, spread):
    size = work.shape[0]

    def wide(value):
        return jnp.broadcast_to(value, (PANEL, size))

    def twice(value):
        return jnp.concatenate([value, value], axis=1)

    here = work[:PANEL, :]
    for start in range(0, size, PANEL):
        after, behind = start + PANEL, start + 2 * PANEL
        place = (start // PANEL % 2) * PANEL * PANEL
        for k in range(PANEL):
            lines = slice(place + k * PANEL, place + (k + 1) * PANEL)
            spread[lines, :] = wide(here[:, start + k : start + k + 1])
        block = {
            (i, k): wide(spread[place + k * PANEL + i : place + k * PANEL + i + 1, :])
            for i in range(PANEL)
            for k in range(i, PANEL)
        }
        lines = [
            jnp.broadcast_to(work[start + i : start + i + 1, :], (PANEL, 2 * size))
            for i in range(PANEL)
        ]
        below, columns = None, []
        if after < size:
            below = work[after:behind, :]
            columns = [wide(below[:, start + k : start + k + 1]) for k in range(PANEL)]
        for j in range(PANEL):
            scale = lax.rsqrt(block[j, j])
            line = lines[j] * twice(scale)
            rows[start + j : start + j + 1, :] = line[:1]
            times = {i: block[j, i] * scale for i in range(j + 1, PANEL)}
            for i, factor in times.items():
                lines[i] = lines[i] - twice(factor) * line
                for k in range(i, PANEL):
                    block[i, k] = block[i, k] - factor * times[k]
            if columns:
                factor = columns[j] * scale
                for k in range(j + 1, PANEL):
                    columns[k] = columns[k] - factor * times[k]
                below = below - twice(factor) * line
        if after < size:
            work[after:behind, :] = below
        if behind < size:
            high, mid, low = [part.astype(F32) for part in split3(rows[start:after, :])]
            left = jnp.concatenate([high, high, mid, high, low, mid], axis=0)[:, :size]
            right = jnp.concatenate([high, mid, high, low, high, mid], axis=0)
            update = lax.dot_general(
                left.astype(BF16),
                right.astype(BF16),
                (((0,), (0,)), ((), ())),
                preferred_element_type=F32,
            )
            work[behind:, :] = work[behind:, :] - update[behind:, :]
        here = below


def finish_kernel(points, own, theirs, parts, out, work, rows, spread, result, sems):
    some, size = own.shape
    begin = lax.rem(lax.axis_index("lmk"), 2) * some
    work[pl.ds(pl.multiple_of(begin, some), some), :size] = own[...] / points
    work[pl.ds(pl.multiple_of(some - begin, some), some), :size] = theirs[...] / points
    work[:, size:] = jnp.where(eye(size), 1.0, 0.0)
    eliminate(work, rows, spread)
    high, low, _ = split3(rows[:, size:])
    right = jnp.concatenate([high, low, high], axis=1)
    copies = []
    for start in range(0, parts.shape[0], TILE):
        lines = pl.ds(start, min(TILE, parts.shape[0] - start))
        result[lines, :] = lax.dot_general(
            parts[lines, :], right, (((1,), (1,)), ((), ())), preferred_element_type=F32
        )
        copies.append(
            pltpu.make_async_copy(result.at[lines], out.at[lines], sems.at[len(copies)])
        )
        copies[-1].start()
    for copy in copies:
        copy.wait()


def per_device(points, landmarks, eigvecs):
    num_pts = lax.axis_size("pts")
    num_lmk = lax.axis_size("lmk")
    num_rows, features = points.shape
    size = eigvecs.shape[1]
    half = num_rows // 2
    pts_bits = [1 << b for b in reversed(range(num_pts.bit_length() - 1))]
    lmk_bits = [1 << b for b in range(1, num_lmk.bit_length() - 1)]
    shape = jax.ShapeDtypeStruct

    own = (landmarks, eigvecs)
    joined = shape((landmarks.shape[0], features + size), BF16)
    held = {}
    if num_pts == 8:
        held[4] = [swap(value, "pts", num_pts, 4) for value in own]
    held[0] = pl.pallas_call(
        beside_kernel,
        out_shape=joined,
        in_specs=[pl.BlockSpec(memory_space=pltpu.HBM)] * 2,
        out_specs=VMEM,
        scratch_shapes=[pltpu.SemaphoreType.DMA((1 + landmarks.shape[0] // 16,))],
    )(*own)
    if num_pts == 8:
        rounds = [[(0, 4), (0, 2), (0, 1)], [(4, 2), (4, 1)], [(6, 1)]]
        late = (1, 2)
    else:
        rounds, order, late = [], [0], None
        for bit in pts_bits:
            rounds.append([(mask, bit) for mask in order])
            order = order + [mask ^ bit for mask in order]

    flops = 8 * num_rows * landmarks.shape[0] * (features + 2 * size)

    def more(total, masks):
        return call_on(
            functools.partial(next_kernel, len(masks)),
            shape((num_rows, 2 * size), F32),
            (unit, *[held[mask] for mask in masks], total),
            aliases={len(masks) + 1: 0},
            flops=flops * len(masks),
        )

    ready, unit, total = [0], None, None
    for turn, hops in enumerate(rounds):
        for mask, bit in hops:
            if mask ^ bit in held:
                continue
            held[mask ^ bit] = swap(held[mask], "pts", num_pts, bit)
        if unit is None:
            unit, total = call_on(
                first_kernel,
                (shape((num_rows, features), BF16), shape((num_rows, 2 * size), F32)),
                (points, held[0]),
                flops=flops * 4,
            )
        else:
            total = more(total, ready)
        ready = [mask ^ bit for mask, bit in hops]
        if turn == 1 and late:
            mask, bit = late
            held[mask], total = lax.optimization_barrier((held[mask], total))
            held[mask ^ bit] = swap(held[mask], "pts", num_pts, bit)
        if turn + 1 < len(rounds):
            sources = [mask for mask, _ in rounds[turn + 1]]
            tied = list(dict.fromkeys(ready + sources))[::-1]
            *fresh, total = lax.optimization_barrier((*[held[mask] for mask in tied], total))
            held.update(zip(tied, fresh))
            if turn == 0 and late:
                held[4] = call_on(join_kernel, joined, held[4])
    if late:
        total = more(total, [late[0] ^ late[1]])
    group = ready
    extra = -(-(half // LANES) // 8) * 8
    send, keep = [
        call_on(
            functools.partial(last_kernel, len(group), mine),
            shape((half + extra, size), F32),
            (unit, *[held[mask] for mask in group], total),
            scratch=[pltpu.VMEM((half, 2 * size), F32)],
            flops=flops * len(group) // 2,
        )
        for mine in (False, True)
    ]
    packed = shape((half + 4 * extra, size), BF16)
    mine = call_on(
        functools.partial(pack_kernel, half), packed, (keep, swap(send, "lmk", num_lmk, 1))
    )
    for bit in lmk_bits[:-1]:
        mine = call_on(
            functools.partial(repack_kernel, half), packed, (mine, swap(mine, "lmk", num_lmk, bit))
        )
    embed, part, send = call_on(
        functools.partial(gram_kernel, half),
        (shape((half, size), F32), *[shape((size // 2, size), F32)] * 2),
        (mine, swap(mine, "lmk", num_lmk, lmk_bits[-1])),
        scratch=[pltpu.VMEM((size, size), F32)],
    )
    part = part + swap(send, "lmk", num_lmk, 1)
    parts = call_on(
        parts_kernel,
        shape((num_rows, 3 * size), BF16),
        (embed, swap(embed, "lmk", num_lmk, 1)),
    )
    if num_pts == 8:
        pair = part + swap(part, "pts", num_pts, 1)
        part = pair + (swap(part, "pts", num_pts, 2) + swap(part, "pts", num_pts, 3))
        pts_bits = [4]
    for bit in pts_bits:
        part = part + swap(part, "pts", num_pts, bit)
    return call_on(
        functools.partial(finish_kernel, float(num_rows * num_pts)),
        shape((num_rows, size), F32),
        (part, swap(part, "lmk", num_lmk, 1), parts),
        scratch=[
            *[pltpu.VMEM((size, 2 * size), F32)] * 2,
            pltpu.VMEM((2 * PANEL * PANEL, size), F32),
            pltpu.VMEM((num_rows, size), F32),
            pltpu.SemaphoreType.DMA((-(-num_rows // TILE),)),
        ],
        out_specs=pl.BlockSpec(memory_space=pltpu.HBM),
    )


def solution(mesh):
    placed = (P("pts", None), P(("pts", "lmk"), None), P(("pts", "lmk"), None))
    return jax.shard_map(
        per_device, mesh=mesh, in_specs=placed, out_specs=P("pts", None), check_vma=False
    )
```

```python
import functools
import math

import jax
import jax.numpy as jnp
from jax import lax
from jax.experimental import pallas as pl
from jax.experimental.pallas import tpu as pltpu
from jax.sharding import PartitionSpec as P

kernel_gain = 16.0
LANES = 128
TILE = 512
PANEL = 8
VMEM = pl.BlockSpec(memory_space=pltpu.VMEM)
BF16 = jnp.bfloat16
F32 = jnp.float32


def unit_rows(values):
    floats = values.astype(F32)
    factor = lax.rsqrt(jnp.mean(floats * floats, axis=-1, keepdims=True) + 1e-06) / math.sqrt(
        values.shape[-1]
    )
    return (floats * factor).astype(BF16)


def split3(value):
    high = value.astype(BF16)
    rest = value - high.astype(F32)
    mid = rest.astype(BF16)
    low = (rest - mid.astype(F32)).astype(BF16)
    return high, mid, low


def swap(value, axis, size, bit):
    return lax.ppermute(value, axis, [(i, i ^ bit) for i in range(size)])


def eye(size):
    row = lax.broadcasted_iota(jnp.int32, (size, size), 0)
    column = lax.broadcasted_iota(jnp.int32, (size, size), 1)
    return row == column


def call_on(kernel, out, operands, **rest):
    return pl.pallas_call(
        kernel,
        out_shape=out,
        in_specs=[rest.get("in_specs", VMEM)] * len(operands),
        out_specs=rest.get("out_specs", jax.tree.map(lambda _: VMEM, out)),
        scratch_shapes=rest.get("scratch", ()),
        input_output_aliases=rest.get("aliases", {}),
        cost_estimate=pl.CostEstimate(
            flops=rest.get("flops", 0), bytes_accessed=1 << 20, transcendentals=0
        ),
        compiler_params=pltpu.CompilerParams(vmem_limit_bytes=48 << 20),
    )(*operands)


def beside_kernel(left, right, out, sems):
    width = left.shape[1]
    copies = [pltpu.make_async_copy(right, out.at[:, width:], sems.at[0])]
    for start in range(0, left.shape[0], 16):
        rows = pl.ds(start, 16)
        copies.append(
            pltpu.make_async_copy(left.at[rows], out.at[rows, :width], sems.at[len(copies)])
        )
    for copy in copies:
        copy.start()
    for copy in copies:
        copy.wait()


def meet(unit, blocks, before, total, begin=0):
    features = unit.shape[1]
    lands = jnp.concatenate([unit_rows(block[:, :features]) for block in blocks], axis=0)
    vectors = jnp.concatenate([block[:, features:] for block in blocks], axis=0)
    vectors = jnp.concatenate([vectors, jnp.ones_like(vectors)], axis=1)
    lands = lands.T
    for start in range(0, total.shape[0], TILE):
        size = min(TILE, total.shape[0] - start)
        rows = pl.ds(start, size)
        cosine = jnp.dot(
            unit[pl.ds(begin + start, size), :], lands, preferred_element_type=F32
        )
        kernel = jnp.exp(2.0 * kernel_gain * (cosine - 1.0)).astype(BF16)
        more = jnp.dot(kernel, vectors, preferred_element_type=F32)
        if before is not None:
            more = more + before[pl.ds(begin + start, size), :]
        total[rows, :] = more


def first_kernel(points, block, unit, total):
    for start in range(0, points.shape[0], TILE):
        rows = slice(start, start + TILE)
        unit[rows, :] = unit_rows(points[rows, :])
    meet(unit, [block], None, total)


def next_kernel(count, unit, *refs):
    blocks, before, total = refs[:count], refs[count], refs[count + 1]
    meet(unit, blocks, before, total)


def last_kernel(count, mine, unit, *refs):
    blocks, before, out, total = refs[:count], *refs[count:]
    half = total.shape[0]
    core = lax.rem(lax.axis_index("lmk"), 2)
    begin = core * half if mine else half - core * half
    meet(unit, blocks, before, total, pl.multiple_of(begin, half))
    out[:half, :] = total[:, :LANES]
    diagonal = eye(LANES)
    lines = []
    for start in range(0, half, LANES):
        wide = total[start : start + LANES, LANES:]
        lines.append(jnp.sum(jnp.where(diagonal, wide, 0.0), axis=0, keepdims=True))
    lines += [jnp.ones_like(lines[0])] * (-len(lines) % 8)
    out[half:, :] = jnp.concatenate(lines, axis=0)


def pack(value, half, out):
    out[:half, :] = value[:half, :].astype(BF16)
    tail = value[half:, :]
    parts = [part for part in split3(tail)]
    parts.append(jnp.zeros_like(parts[0]))
    out[half:, :] = jnp.concatenate([part.astype(F32) for part in parts], axis=0).astype(BF16)


def unpack(packed, half):
    value = packed[...].astype(F32)
    some = (value.shape[0] - half) // 4
    tail = value[half:, :]
    degree = (tail[2 * some : 3 * some] + tail[some : 2 * some]) + tail[:some]
    return value[:half], degree


def pack_kernel(half, mine, other, out):
    pack(mine[...] + other[...], half, out)


def repack_kernel(half, mine, other, out):
    value, degree = unpack(mine, half)
    more, plus = unpack(other, half)
    pack(jnp.concatenate([value + more, degree + plus], axis=0), half, out)


def gram_kernel(half, mine, other, embed, keep, send, gram):
    value, degree = unpack(mine, half)
    more, plus = unpack(other, half)
    projected = value + more
    scale = lax.rsqrt(degree + plus)
    diagonal = eye(LANES)
    for block in range(half // LANES):
        rows = slice(block * LANES, (block + 1) * LANES)
        line = jnp.broadcast_to(scale[block : block + 1, :], (LANES, LANES))
        column = jnp.sum(jnp.where(diagonal, line, 0.0), axis=1, keepdims=True)
        embed[rows, :] = projected[rows, :] * column
    gram[...] = lax.dot_general(
        embed[...],
        embed[...],
        (((0,), (0,)), ((), ())),
        precision=lax.Precision.HIGHEST,
        preferred_element_type=F32,
    )
    some = keep.shape[0]
    begin = lax.rem(lax.axis_index("lmk"), 2) * some
    keep[...] = gram[pl.ds(pl.multiple_of(begin, some), some), :]
    send[...] = gram[pl.ds(pl.multiple_of(some - begin, some), some), :]


def parts_kernel(own, theirs, out):
    half = own.shape[0]
    core = lax.rem(lax.axis_index("lmk"), 2)
    for embed, begin in ((own, core * half), (theirs, half - core * half)):
        high, low, _ = split3(embed[...])
        out[pl.ds(pl.multiple_of(begin, half), half), :] = jnp.concatenate(
            [high, high, low], axis=1
        )


def eliminate(work, rows, spread):
    size = work.shape[0]

    def wide(value):
        return jnp.broadcast_to(value, (PANEL, size))

    def twice(value):
        return jnp.concatenate([value, value], axis=1)

    here = work[:PANEL, :]
    for start in range(0, size, PANEL):
        after, behind = start + PANEL, start + 2 * PANEL
        place = (start // PANEL % 2) * PANEL * PANEL
        for k in range(PANEL):
            lines = slice(place + k * PANEL, place + (k + 1) * PANEL)
            spread[lines, :] = wide(here[:, start + k : start + k + 1])
        block = {
            (i, k): wide(spread[place + k * PANEL + i : place + k * PANEL + i + 1, :])
            for i in range(PANEL)
            for k in range(i, PANEL)
        }
        lines = [
            jnp.broadcast_to(work[start + i : start + i + 1, :], (PANEL, 2 * size))
            for i in range(PANEL)
        ]
        below, columns = None, []
        if after < size:
            below = work[after:behind, :]
            columns = [wide(below[:, start + k : start + k + 1]) for k in range(PANEL)]
        for j in range(PANEL):
            scale = lax.rsqrt(block[j, j])
            line = lines[j] * twice(scale)
            rows[start + j : start + j + 1, :] = line[:1]
            times = {i: block[j, i] * scale for i in range(j + 1, PANEL)}
            for i, factor in times.items():
                lines[i] = lines[i] - twice(factor) * line
                for k in range(i, PANEL):
                    block[i, k] = block[i, k] - factor * times[k]
            if columns:
                factor = columns[j] * scale
                for k in range(j + 1, PANEL):
                    columns[k] = columns[k] - factor * times[k]
                below = below - twice(factor) * line
        if after < size:
            work[after:behind, :] = below
        if behind < size:
            high, mid, low = [part.astype(F32) for part in split3(rows[start:after, :])]
            left = jnp.concatenate([high, high, mid, high, low, mid], axis=0)[:, :size]
            right = jnp.concatenate([high, mid, high, low, high, mid], axis=0)
            update = lax.dot_general(
                left.astype(BF16),
                right.astype(BF16),
                (((0,), (0,)), ((), ())),
                preferred_element_type=F32,
            )
            work[behind:, :] = work[behind:, :] - update[behind:, :]
        here = below


def finish_kernel(points, own, theirs, parts, out, work, rows, spread, result, sems):
    some, size = own.shape
    begin = lax.rem(lax.axis_index("lmk"), 2) * some
    work[pl.ds(pl.multiple_of(begin, some), some), :size] = own[...] / points
    work[pl.ds(pl.multiple_of(some - begin, some), some), :size] = theirs[...] / points
    work[:, size:] = jnp.where(eye(size), 1.0, 0.0)
    eliminate(work, rows, spread)
    high, low, _ = split3(rows[:, size:])
    right = jnp.concatenate([high, low, high], axis=1)
    copies = []
    for start in range(0, parts.shape[0], TILE):
        lines = pl.ds(start, min(TILE, parts.shape[0] - start))
        result[lines, :] = lax.dot_general(
            parts[lines, :], right, (((1,), (1,)), ((), ())), preferred_element_type=F32
        )
        copies.append(
            pltpu.make_async_copy(result.at[lines], out.at[lines], sems.at[len(copies)])
        )
        copies[-1].start()
    for copy in copies:
        copy.wait()


def per_device(points, landmarks, eigvecs):
    num_pts = lax.axis_size("pts")
    num_lmk = lax.axis_size("lmk")
    num_rows, features = points.shape
    size = eigvecs.shape[1]
    half = num_rows // 2
    pts_bits = [1 << b for b in reversed(range(num_pts.bit_length() - 1))]
    lmk_bits = [1 << b for b in range(1, num_lmk.bit_length() - 1)]
    shape = jax.ShapeDtypeStruct

    held = {
        0: pl.pallas_call(
            beside_kernel,
            out_shape=shape((landmarks.shape[0], features + size), BF16),
            in_specs=[pl.BlockSpec(memory_space=pltpu.HBM)] * 2,
            out_specs=VMEM,
            scratch_shapes=[pltpu.SemaphoreType.DMA((1 + landmarks.shape[0] // 16,))],
        )(landmarks, eigvecs)
    }
    if num_pts == 8:
        rounds = [[(0, 4), (0, 2), (0, 1)], [(4, 2), (4, 1)], [(6, 1)]]
        late = (1, 2)
    else:
        rounds, order, late = [], [0], None
        for bit in pts_bits:
            rounds.append([(mask, bit) for mask in order])
            order = order + [mask ^ bit for mask in order]

    flops = 8 * num_rows * landmarks.shape[0] * (features + 2 * size)

    def more(total, masks):
        return call_on(
            functools.partial(next_kernel, len(masks)),
            shape((num_rows, 2 * size), F32),
            (unit, *[held[mask] for mask in masks], total),
            aliases={len(masks) + 1: 0},
            flops=flops * len(masks),
        )

    ready, unit, total = [0], None, None
    for turn, hops in enumerate(rounds):
        for mask, bit in hops:
            held[mask ^ bit] = swap(held[mask], "pts", num_pts, bit)
        if unit is None:
            unit, total = call_on(
                first_kernel,
                (shape((num_rows, features), BF16), shape((num_rows, 2 * size), F32)),
                (points, held[0]),
                flops=flops,
            )
        else:
            total = more(total, ready)
        ready = [mask ^ bit for mask, bit in hops]
        if turn == 1 and late:
            mask, bit = late
            held[mask], total = lax.optimization_barrier((held[mask], total))
            held[mask ^ bit] = swap(held[mask], "pts", num_pts, bit)
        if turn + 1 < len(rounds):
            sources = [mask for mask, _ in rounds[turn + 1]]
            tied = list(dict.fromkeys(ready + sources))[::-1]
            *fresh, total = lax.optimization_barrier((*[held[mask] for mask in tied], total))
            held.update(zip(tied, fresh))
    if late:
        total = more(total, [late[0] ^ late[1]])
    group = ready
    extra = -(-(half // LANES) // 8) * 8
    send, keep = [
        call_on(
            functools.partial(last_kernel, len(group), mine),
            shape((half + extra, size), F32),
            (unit, *[held[mask] for mask in group], total),
            scratch=[pltpu.VMEM((half, 2 * size), F32)],
            flops=flops * len(group) // 2,
        )
        for mine in (False, True)
    ]
    packed = shape((half + 4 * extra, size), BF16)
    mine = call_on(
        functools.partial(pack_kernel, half), packed, (keep, swap(send, "lmk", num_lmk, 1))
    )
    for bit in lmk_bits[:-1]:
        mine = call_on(
            functools.partial(repack_kernel, half), packed, (mine, swap(mine, "lmk", num_lmk, bit))
        )
    embed, part, send = call_on(
        functools.partial(gram_kernel, half),
        (shape((half, size), F32), *[shape((size // 2, size), F32)] * 2),
        (mine, swap(mine, "lmk", num_lmk, lmk_bits[-1])),
        scratch=[pltpu.VMEM((size, size), F32)],
    )
    part = part + swap(send, "lmk", num_lmk, 1)
    parts = call_on(
        parts_kernel,
        shape((num_rows, 3 * size), BF16),
        (embed, swap(embed, "lmk", num_lmk, 1)),
    )
    if num_pts == 8:
        pair = part + swap(part, "pts", num_pts, 1)
        part = pair + (swap(part, "pts", num_pts, 2) + swap(part, "pts", num_pts, 3))
        pts_bits = [4]
    for bit in pts_bits:
        part = part + swap(part, "pts", num_pts, bit)
    return call_on(
        functools.partial(finish_kernel, float(num_rows * num_pts)),
        shape((num_rows, size), F32),
        (part, swap(part, "lmk", num_lmk, 1), parts),
        scratch=[
            *[pltpu.VMEM((size, 2 * size), F32)] * 2,
            pltpu.VMEM((2 * PANEL * PANEL, size), F32),
            pltpu.VMEM((num_rows, size), F32),
            pltpu.SemaphoreType.DMA((-(-num_rows // TILE),)),
        ],
        out_specs=pl.BlockSpec(memory_space=pltpu.HBM),
    )


def solution(mesh):
    placed = (P("pts", None), P(("pts", "lmk"), None), P(("pts", "lmk"), None))
    return jax.shard_map(
        per_device, mesh=mesh, in_specs=placed, out_specs=P("pts", None), check_vma=False
    )
```

```python
import functools
import math

import jax
import jax.numpy as jnp
from jax import lax
from jax.experimental import pallas as pl
from jax.experimental.pallas import tpu as pltpu
from jax.sharding import PartitionSpec as P

kernel_gain = 16.0
LANES = 128
TILE = 512
PANEL = 8
VMEM = pl.BlockSpec(memory_space=pltpu.VMEM)
BF16 = jnp.bfloat16
F32 = jnp.float32


def unit_rows(values):
    floats = values.astype(F32)
    factor = lax.rsqrt(jnp.mean(floats * floats, axis=-1, keepdims=True) + 1e-06) / math.sqrt(
        values.shape[-1]
    )
    return (floats * factor).astype(BF16)


def split3(value):
    high = value.astype(BF16)
    rest = value - high.astype(F32)
    mid = rest.astype(BF16)
    low = (rest - mid.astype(F32)).astype(BF16)
    return high, mid, low


def swap(value, axis, size, bit):
    return lax.ppermute(value, axis, [(i, i ^ bit) for i in range(size)])


def eye(size):
    row = lax.broadcasted_iota(jnp.int32, (size, size), 0)
    column = lax.broadcasted_iota(jnp.int32, (size, size), 1)
    return row == column


def call_on(kernel, out, operands, **rest):
    return pl.pallas_call(
        kernel,
        out_shape=out,
        in_specs=[rest.get("in_specs", VMEM)] * len(operands),
        out_specs=rest.get("out_specs", jax.tree.map(lambda _: VMEM, out)),
        scratch_shapes=rest.get("scratch", ()),
        input_output_aliases=rest.get("aliases", {}),
        cost_estimate=pl.CostEstimate(
            flops=rest.get("flops", 0), bytes_accessed=1 << 20, transcendentals=0
        ),
        compiler_params=pltpu.CompilerParams(vmem_limit_bytes=48 << 20),
    )(*operands)


def beside_kernel(left, right, out, sems):
    width = left.shape[1]
    copies = [pltpu.make_async_copy(right, out.at[:, width:], sems.at[0])]
    for start in range(0, left.shape[0], 16):
        rows = pl.ds(start, 16)
        copies.append(
            pltpu.make_async_copy(left.at[rows], out.at[rows, :width], sems.at[len(copies)])
        )
    for copy in copies:
        copy.start()
    for copy in copies:
        copy.wait()


def meet(unit, blocks, before, total, begin=0):
    features = unit.shape[1]
    lands = jnp.concatenate([unit_rows(block[:, :features]) for block in blocks], axis=0)
    vectors = jnp.concatenate([block[:, features:] for block in blocks], axis=0)
    vectors = jnp.concatenate([vectors, jnp.ones_like(vectors)], axis=1)
    lands = lands.T
    for start in range(0, total.shape[0], TILE):
        size = min(TILE, total.shape[0] - start)
        rows = pl.ds(start, size)
        cosine = jnp.dot(
            unit[pl.ds(begin + start, size), :], lands, preferred_element_type=F32
        )
        kernel = jnp.exp(2.0 * kernel_gain * (cosine - 1.0)).astype(BF16)
        more = jnp.dot(kernel, vectors, preferred_element_type=F32)
        if before is not None:
            more = more + before[pl.ds(begin + start, size), :]
        total[rows, :] = more


def first_kernel(points, block, unit, total):
    for start in range(0, points.shape[0], TILE):
        rows = slice(start, start + TILE)
        unit[rows, :] = unit_rows(points[rows, :])
    meet(unit, [block], None, total)


def next_kernel(count, unit, *refs):
    blocks, before, total = refs[:count], refs[count], refs[count + 1]
    meet(unit, blocks, before, total)


def last_kernel(count, mine, unit, *refs):
    blocks, before, out, total = refs[:count], *refs[count:]
    half = total.shape[0]
    core = lax.rem(lax.axis_index("lmk"), 2)
    begin = core * half if mine else half - core * half
    meet(unit, blocks, before, total, pl.multiple_of(begin, half))
    out[:half, :] = total[:, :LANES]
    diagonal = eye(LANES)
    lines = []
    for start in range(0, half, LANES):
        wide = total[start : start + LANES, LANES:]
        lines.append(jnp.sum(jnp.where(diagonal, wide, 0.0), axis=0, keepdims=True))
    lines += [jnp.ones_like(lines[0])] * (-len(lines) % 8)
    out[half:, :] = jnp.concatenate(lines, axis=0)


def pack(value, half, out):
    out[:half, :] = value[:half, :].astype(BF16)
    tail = value[half:, :]
    parts = [part for part in split3(tail)]
    parts.append(jnp.zeros_like(parts[0]))
    out[half:, :] = jnp.concatenate([part.astype(F32) for part in parts], axis=0).astype(BF16)


def unpack(packed, half):
    value = packed[...].astype(F32)
    some = (value.shape[0] - half) // 4
    tail = value[half:, :]
    degree = (tail[2 * some : 3 * some] + tail[some : 2 * some]) + tail[:some]
    return value[:half], degree


def pack_kernel(half, mine, other, out):
    pack(mine[...] + other[...], half, out)


def repack_kernel(half, mine, other, out):
    value, degree = unpack(mine, half)
    more, plus = unpack(other, half)
    pack(jnp.concatenate([value + more, degree + plus], axis=0), half, out)


def gram_kernel(half, mine, other, embed, keep, send, gram):
    value, degree = unpack(mine, half)
    more, plus = unpack(other, half)
    projected = value + more
    scale = lax.rsqrt(degree + plus)
    diagonal = eye(LANES)
    for block in range(half // LANES):
        rows = slice(block * LANES, (block + 1) * LANES)
        line = jnp.broadcast_to(scale[block : block + 1, :], (LANES, LANES))
        column = jnp.sum(jnp.where(diagonal, line, 0.0), axis=1, keepdims=True)
        embed[rows, :] = projected[rows, :] * column
    gram[...] = lax.dot_general(
        embed[...],
        embed[...],
        (((0,), (0,)), ((), ())),
        precision=lax.Precision.HIGHEST,
        preferred_element_type=F32,
    )
    some = keep.shape[0]
    begin = lax.rem(lax.axis_index("lmk"), 2) * some
    keep[...] = gram[pl.ds(pl.multiple_of(begin, some), some), :]
    send[...] = gram[pl.ds(pl.multiple_of(some - begin, some), some), :]


def parts_kernel(own, theirs, out):
    half = own.shape[0]
    core = lax.rem(lax.axis_index("lmk"), 2)
    for embed, begin in ((own, core * half), (theirs, half - core * half)):
        high, low, _ = split3(embed[...])
        out[pl.ds(pl.multiple_of(begin, half), half), :] = jnp.concatenate(
            [high, high, low], axis=1
        )


def eliminate(work, rows, spread):
    size = work.shape[0]

    def wide(value):
        return jnp.broadcast_to(value, (PANEL, size))

    def twice(value):
        return jnp.concatenate([value, value], axis=1)

    here = work[:PANEL, :]
    for start in range(0, size, PANEL):
        after, behind = start + PANEL, start + 2 * PANEL
        place = (start // PANEL % 2) * PANEL * PANEL
        for k in range(PANEL):
            lines = slice(place + k * PANEL, place + (k + 1) * PANEL)
            spread[lines, :] = wide(here[:, start + k : start + k + 1])
        block = {
            (i, k): wide(spread[place + k * PANEL + i : place + k * PANEL + i + 1, :])
            for i in range(PANEL)
            for k in range(i, PANEL)
        }
        lines = [
            jnp.broadcast_to(work[start + i : start + i + 1, :], (PANEL, 2 * size))
            for i in range(PANEL)
        ]
        below, columns = None, []
        if after < size:
            below = work[after:behind, :]
            columns = [wide(below[:, start + k : start + k + 1]) for k in range(PANEL)]
        for j in range(PANEL):
            scale = lax.rsqrt(block[j, j])
            line = lines[j] * twice(scale)
            rows[start + j : start + j + 1, :] = line[:1]
            times = {i: block[j, i] * scale for i in range(j + 1, PANEL)}
            for i, factor in times.items():
                lines[i] = lines[i] - twice(factor) * line
                for k in range(i, PANEL):
                    block[i, k] = block[i, k] - factor * times[k]
            if columns:
                factor = columns[j] * scale
                for k in range(j + 1, PANEL):
                    columns[k] = columns[k] - factor * times[k]
                below = below - twice(factor) * line
        if after < size:
            work[after:behind, :] = below
        if behind < size:
            high, mid, low = [part.astype(F32) for part in split3(rows[start:after, :])]
            left = jnp.concatenate([high, high, mid, high, low, mid], axis=0)[:, :size]
            right = jnp.concatenate([high, mid, high, low, high, mid], axis=0)
            update = lax.dot_general(
                left.astype(BF16),
                right.astype(BF16),
                (((0,), (0,)), ((), ())),
                preferred_element_type=F32,
            )
            work[behind:, :] = work[behind:, :] - update[behind:, :]
        here = below


def finish_kernel(points, own, theirs, parts, out, work, rows, spread, result, sems):
    some, size = own.shape
    begin = lax.rem(lax.axis_index("lmk"), 2) * some
    work[pl.ds(pl.multiple_of(begin, some), some), :size] = own[...] / points
    work[pl.ds(pl.multiple_of(some - begin, some), some), :size] = theirs[...] / points
    work[:, size:] = jnp.where(eye(size), 1.0, 0.0)
    eliminate(work, rows, spread)
    high, low, _ = split3(rows[:, size:])
    right = jnp.concatenate([high, low, high], axis=1)
    copies = []
    for start in range(0, parts.shape[0], TILE):
        lines = pl.ds(start, min(TILE, parts.shape[0] - start))
        result[lines, :] = lax.dot_general(
            parts[lines, :], right, (((1,), (1,)), ((), ())), preferred_element_type=F32
        )
        copies.append(
            pltpu.make_async_copy(result.at[lines], out.at[lines], sems.at[len(copies)])
        )
        copies[-1].start()
    for copy in copies:
        copy.wait()


def per_device(points, landmarks, eigvecs):
    num_pts = lax.axis_size("pts")
    num_lmk = lax.axis_size("lmk")
    num_rows, features = points.shape
    size = eigvecs.shape[1]
    half = num_rows // 2
    pts_bits = [1 << b for b in reversed(range(num_pts.bit_length() - 1))]
    lmk_bits = [1 << b for b in range(1, num_lmk.bit_length() - 1)]
    shape = jax.ShapeDtypeStruct

    held = {
        0: pl.pallas_call(
            beside_kernel,
            out_shape=shape((landmarks.shape[0], features + size), BF16),
            in_specs=[pl.BlockSpec(memory_space=pltpu.HBM)] * 2,
            out_specs=VMEM,
            scratch_shapes=[pltpu.SemaphoreType.DMA((1 + landmarks.shape[0] // 16,))],
        )(landmarks, eigvecs)
    }
    if num_pts == 8:
        rounds = [[(0, 4), (0, 2), (0, 1)], [(4, 2), (4, 1)], [(6, 1)]]
        late = (1, 2)
    else:
        rounds, order, late = [], [0], None
        for bit in pts_bits:
            rounds.append([(mask, bit) for mask in order])
            order = order + [mask ^ bit for mask in order]

    flops = 8 * num_rows * landmarks.shape[0] * (features + 2 * size)

    def more(total, masks):
        return call_on(
            functools.partial(next_kernel, len(masks)),
            shape((num_rows, 2 * size), F32),
            (unit, *[held[mask] for mask in masks], total),
            aliases={len(masks) + 1: 0},
            flops=flops * len(masks),
        )

    ready, unit, total = [0], None, None
    for turn, hops in enumerate(rounds):
        for mask, bit in hops:
            held[mask ^ bit] = swap(held[mask], "pts", num_pts, bit)
        if unit is None:
            unit, total = call_on(
                first_kernel,
                (shape((num_rows, features), BF16), shape((num_rows, 2 * size), F32)),
                (points, held[0]),
                flops=flops,
            )
        else:
            total = more(total, ready)
        ready = [mask ^ bit for mask, bit in hops]
        if turn == 1 and late:
            mask, bit = late
            held[mask], total = lax.optimization_barrier((held[mask], total))
            held[mask ^ bit] = swap(held[mask], "pts", num_pts, bit)
        if turn + 1 < len(rounds):
            sources = [mask for mask, _ in rounds[turn + 1]]
            tied = list(dict.fromkeys(ready + sources))[::-1]
            *fresh, total = lax.optimization_barrier((*[held[mask] for mask in tied], total))
            held.update(zip(tied, fresh))
    if late:
        total = more(total, [late[0] ^ late[1]])
    group = ready
    extra = -(-(half // LANES) // 8) * 8
    send, keep = [
        call_on(
            functools.partial(last_kernel, len(group), mine),
            shape((half + extra, size), F32),
            (unit, *[held[mask] for mask in group], total),
            scratch=[pltpu.VMEM((half, 2 * size), F32)],
            flops=flops * len(group) // 2,
        )
        for mine in (False, True)
    ]
    packed = shape((half + 4 * extra, size), BF16)
    mine = call_on(
        functools.partial(pack_kernel, half), packed, (keep, swap(send, "lmk", num_lmk, 1))
    )
    for bit in lmk_bits[:-1]:
        mine = call_on(
            functools.partial(repack_kernel, half), packed, (mine, swap(mine, "lmk", num_lmk, bit))
        )
    embed, part, send = call_on(
        functools.partial(gram_kernel, half),
        (shape((half, size), F32), *[shape((size // 2, size), F32)] * 2),
        (mine, swap(mine, "lmk", num_lmk, lmk_bits[-1])),
        scratch=[pltpu.VMEM((size, size), F32)],
    )
    part = part + swap(send, "lmk", num_lmk, 1)
    parts = call_on(
        parts_kernel,
        shape((num_rows, 3 * size), BF16),
        (embed, swap(embed, "lmk", num_lmk, 1)),
    )
    if num_pts == 8:
        part = part + swap(part, "pts", num_pts, 4)
        pair = part + swap(part, "pts", num_pts, 1)
        part = pair + (swap(part, "pts", num_pts, 2) + swap(part, "pts", num_pts, 3))
        pts_bits = []
    for bit in pts_bits:
        part = part + swap(part, "pts", num_pts, bit)
    return call_on(
        functools.partial(finish_kernel, float(num_rows * num_pts)),
        shape((num_rows, size), F32),
        (part, swap(part, "lmk", num_lmk, 1), parts),
        scratch=[
            *[pltpu.VMEM((size, 2 * size), F32)] * 2,
            pltpu.VMEM((2 * PANEL * PANEL, size), F32),
            pltpu.VMEM((num_rows, size), F32),
            pltpu.SemaphoreType.DMA((-(-num_rows // TILE),)),
        ],
        out_specs=pl.BlockSpec(memory_space=pltpu.HBM),
    )


def solution(mesh):
    placed = (P("pts", None), P(("pts", "lmk"), None), P(("pts", "lmk"), None))
    return jax.shard_map(
        per_device, mesh=mesh, in_specs=placed, out_specs=P("pts", None), check_vma=False
    )
```
